256 devices in a mesh: dom: 32 (over x_lo, z, core), col: 8 (over x_hi, y).
Axes of the slice: x: 4 (x_hi: 2, x_lo: 2; x = x_hi * 2 + x_lo), y: 4, z: 8, core: 2. Of those that a mesh axis runs over, the one named last changes fastest.
Arguments:
- feats: bfloat16 [16384, 256], P('dom', 'col'), may hold values from -6 to 6
- w_first: bfloat16 [256, 256], replicated, may hold values from -0.375 to 0.375
- w_second: bfloat16 [256, 256], replicated, may hold values from -0.375 to 0.375
- block_cols: int32 [128, 32], P('dom'), may hold values from 0 to 127, as said below
- block_count: int32 [128], P('dom'), may hold values from 1 to 32
- block_vals: bfloat16 [128, 32, 128, 128], P('dom', 'col'), may hold values from -0.125 to 0.125
- cotangent: bfloat16 [16384, 256], P('dom', 'col'), may hold values from -6 to 6
Outputs:
- output: float32 [16384, 256], P('dom', 'col')
- grad_first: float32 [256, 256], P(None, 'col')
- grad_second: float32 [256, 256], P(None, 'col')
The draws below stay inside these ranges and needn't reach their ends.
Inputs may be any that keep to these rules, and one draw needn't show every extreme that they name: Each row of block_cols names 32 different column blocks.
All inputs are finite; a program needn't handle non-finite values.
Results may differ from the reference program's by a relative error of at most 0.019.
Values may be sent and summed in bfloat16 or wider, within the bound.
A program may use at most 64 MiB of HBM per device.

```python
import jax
import jax.numpy as jnp
from jax import lax

F = 256
BLK = 128
KMAX = 32
NBLK = 128
NODES = 16384


def draw_block_cols(key, part):
    row_ids = jnp.arange(NBLK, dtype=jnp.int32)[:, None]
    col_ids = jnp.arange(NBLK, dtype=jnp.int32)[None, :]
    distance = jnp.minimum((col_ids - row_ids) % NBLK, (row_ids - col_ids) % NBLK)
    inband = (distance <= 16).astype(jnp.int32)
    noise = jax.random.randint(jax.random.fold_in(key, 11), (NBLK, NBLK), 0, 1 << 16)
    base = noise * NBLK + col_ids
    near_scores = inband * (1 << 28) + base
    far_scores = (1 - inband) * (1 << 28) + base
    near_vals, near_cols = lax.top_k(near_scores, KMAX - 4)
    far_vals, far_cols = lax.top_k(far_scores, 4)
    return jnp.concatenate([near_cols, far_cols], axis=1).astype(jnp.int32)


def draw_block_count(key, part):
    first_key = jax.random.fold_in(key, 21)
    second_key = jax.random.fold_in(key, 22)
    counts = jax.random.randint(first_key, (NBLK,), 1, KMAX + 1)
    where_full = jax.random.randint(second_key, (), 0, NBLK)
    counts = counts.at[where_full].set(KMAX)
    return counts.astype(jnp.int32)


def block_scale(rng, dims, split, low, top_value):
    loudness, own = 1.0, jax.random.fold_in(rng, 6)
    for position, parts in split:
        draws = jnp.exp(jax.random.uniform(jax.random.fold_in(own, position), (parts,), jnp.float32, low / len(split), top_value / len(split)))
        loudness = loudness * jnp.repeat(draws, dims[position] // parts).reshape([-1 if axis == position else 1 for axis in range(len(dims))])
    return loudness


def gaussian(stream_key, extent, scale, reach, cuts=(), kind=jnp.bfloat16):
    level = block_scale(stream_key, extent, cuts, -0.22, 0.18) if cuts else 1.0
    drawn = jax.random.normal(stream_key, extent, jnp.float32) * scale * level
    return jnp.minimum(jnp.maximum(drawn, -reach), reach).astype(kind)


def setup_inputs(seed: int = 0) -> dict:
    keys = jax.random.split(jax.random.key(seed), 8)
    feats = gaussian(keys[0], (NODES, F), 1.0, 6.0, ((0, 32), (1, 8)))
    w_first = gaussian(keys[1], (F, F), F ** -0.5, 0.375)
    w_second = gaussian(keys[2], (F, F), F ** -0.5, 0.375)
    block_cols = draw_block_cols(jax.random.fold_in(keys[7], 71), 0)
    block_count = draw_block_count(jax.random.fold_in(keys[7], 71), 0)
    block_vals = gaussian(keys[5], (NBLK, KMAX, BLK, BLK), (BLK * KMAX // 2) ** -0.5, 0.125, ((0, 32), (1, 8)))
    cotangent = gaussian(keys[6], (NODES, F), 1.0, 6.0, ((0, 32), (1, 8)))
    return {"feats": feats, "w_first": w_first, "w_second": w_second, "block_cols": block_cols, "block_count": block_count, "block_vals": block_vals, "cotangent": cotangent}


def aggregate(prod, block_cols, block_count, block_vals):
    blocks = prod.reshape(NBLK, BLK, F)
    slots = jnp.arange(KMAX)

    def one_row(args):
        cols, count, vals = args
        picked = blocks[cols].astype(jnp.float32)
        mask = (slots < count).astype(jnp.float32)
        return jnp.einsum('kij,kjf->if', vals.astype(jnp.float32) * mask[:, None, None], picked)

    return lax.map(one_row, (block_cols, block_count, block_vals)).reshape(NBLK * BLK, F)


def transpose(grad, block_cols, block_count, block_vals):
    rowgrad = grad.reshape(NBLK, BLK, F).astype(jnp.float32)
    slots = jnp.arange(KMAX)

    def step(total, args):
        cols, count, vals, piece = args
        mask = (slots < count).astype(jnp.float32)
        term = jnp.einsum('kij,if->kjf', vals.astype(jnp.float32) * mask[:, None, None], piece)
        return total.at[cols].add(term), None

    total, unused = lax.scan(step, jnp.zeros((NBLK, BLK, F), jnp.float32), (block_cols, block_count, block_vals, rowgrad))
    return total.reshape(NBLK * BLK, F)


def reference(feats, w_first, w_second, block_cols, block_count, block_vals, cotangent):
    proj_first = jnp.dot(feats, w_first, preferred_element_type=jnp.float32).astype(jnp.bfloat16)
    first = aggregate(proj_first, block_cols, block_count, block_vals)
    hidden = (first * jax.nn.sigmoid(first)).astype(jnp.bfloat16)
    proj_second = jnp.dot(hidden, w_second, preferred_element_type=jnp.float32).astype(jnp.bfloat16)
    output = aggregate(proj_second, block_cols, block_count, block_vals)
    back_second = transpose(cotangent, block_cols, block_count, block_vals).astype(jnp.bfloat16)
    grad_second = jnp.dot(hidden.T, back_second, preferred_element_type=jnp.float32)
    hidden_grad = jnp.dot(back_second, w_second.T, preferred_element_type=jnp.float32)
    sig = jax.nn.sigmoid(first)
    act_grad = (hidden_grad * (sig + first * sig * (1.0 - sig))).astype(jnp.bfloat16)
    back_first = transpose(act_grad, block_cols, block_count, block_vals).astype(jnp.bfloat16)
    grad_first = jnp.dot(feats.T, back_first, preferred_element_type=jnp.float32)
    return (output, grad_first, grad_second)
```

```python
import functools

import jax
import jax.numpy as jnp
from jax import lax
from jax.experimental import pallas as pl
from jax.experimental.pallas import tpu as pltpu
from jax.sharding import PartitionSpec as P

BLK = 128
ROWS = 4
MINE = 4
NBLK = 128
WIDE = 32
F = 256
MESH = pl.DeviceIdType.MESH
BF = jnp.bfloat16
F32 = jnp.float32


def far_first(i):
    return 4 + ((i + 1) // 2) * (1 - 2 * (i % 2))


def nt(a, b):
    return lax.dot_general(a, b, (((1,), (1,)), ((), ())), preferred_element_type=F32)


def kernel(
    cols,
    inv,
    feats_in,
    cot_in,
    w1_cols,
    w2_cols,
    w2_rows,
    vals_in,
    out_ref,
    grads_ref,
    vals,
    feats,
    hid,
    back,
    first,
    v1,
    v2,
    bufs,
    red,
    ssem,
    rvals,
    rcol,
    rgather,
    rred,
    rgrad,
    lsem,
):
    d, c = lax.axis_index("dom"), lax.axis_index("col")
    xlo, z, core = d // 16, (d // 2) % 8, d % 2
    xhi, y = c // 4, c % 4

    def dom_at(xl, zz, cc):
        return (xl * 8 + zz) * 2 + cc

    def col_at(xh, yy):
        return xh * 4 + yy % 4

    up, down = (d, col_at(xhi, y + 1)), (d, col_at(xhi, y + 3))
    across = (d, col_at(1 - xhi, y))
    beside = (dom_at(1 - xlo, z, core), c)
    sibling = (dom_at(xlo, z, 1 - core), c)
    corner = (dom_at(1 - xlo, z, 1 - core), c)

    def along(k):
        return (dom_at(xlo, (z + k) % 8, core), c)

    col_peers = [
        (d, col_at((xhi + a) % 2, y + b)) for a in range(2) for b in range(4) if a + b
    ]

    started = []

    def send(src, dst, sem, to):
        copy = pltpu.make_async_remote_copy(
            src_ref=src,
            dst_ref=dst,
            send_sem=ssem.at[len(started)],
            recv_sem=sem,
            device_id=to,
            device_id_type=MESH,
        )
        copy.start()
        started.append(copy)

    def arrived(dst, sem):
        pltpu.make_async_remote_copy(
            src_ref=dst,
            dst_ref=dst,
            send_sem=ssem.at[0],
            recv_sem=sem,
            device_id=up,
            device_id_type=MESH,
        ).wait_recv()

    barrier = pltpu.get_barrier_semaphore()
    peers = col_peers + [along(k) for k in range(1, 8)] + [beside, sibling, corner]
    for peer in peers:
        pl.semaphore_signal(barrier, inc=1, device_id=peer, device_id_type=MESH)
    pl.semaphore_wait(barrier, len(peers))

    def spread(src, full, which):
        for n, peer in enumerate(col_peers):
            send(src, full.at[c], rcol.at[which, n], peer)

    def collect(full, which):
        for n in range(7):
            arrived(full.at[0], rcol.at[which, n])

    spread(feats_in, feats, 0)

    def part(q, r):
        return vals.at[pl.ds(q * 16 + r * MINE, MINE)]

    own = pltpu.make_async_copy(vals_in, vals.at[pl.ds(c * 16, 16)], lsem)
    own.start()
    for r in range(ROWS):
        src = vals_in.at[pl.ds(r * MINE, MINE)]
        for to in (up, down, across):
            send(src, part(c, r), rvals.at[c, r], to)

    below, above = col_at(xhi, y + 3), col_at(xhi, y + 1)
    partner, opposite = col_at(1 - xhi, y), col_at(xhi, y + 2)
    far_below, far_above = col_at(1 - xhi, y + 3), col_at(1 - xhi, y + 1)
    far_opposite = col_at(1 - xhi, y + 2)

    def take(q, r):
        arrived(part(q, r), rvals.at[q, r])

    def pass_on(q, r, to):
        send(part(q, r), part(q, r), rvals.at[q, r], to)

    def relay(r):
        take(below, r)
        if r < 2:
            pass_on(below, r, up)
        take(above, r)
        if r >= 2:
            pass_on(above, r, down)
        take(partner, r)
        pass_on(partner, r, up)
        pass_on(partner, r, down)

    def cross(r):
        take(opposite, r)
        pass_on(opposite, r, across)

    def at_block(v, xl, zz, cc):
        return v.at[pl.ds(cc * 64 + (xl * 8 + zz) * 4, 4)]

    def gather_start(v, which):
        mine = at_block(v, xlo, z, core)
        for i in range(7):
            send(mine, mine, rgather.at[which, i], along(far_first(i)))
        send(mine, mine, rgather.at[which, 7], beside)

    def gather_relay(v, which):
        for i in range(7):
            zz = (z + 8 - far_first(i)) % 8
            piece = at_block(v, xlo, zz, core)
            arrived(piece, rgather.at[which, i])
            send(piece, piece, rgather.at[which, 8 + i], beside)
        half = v.at[pl.ds(core * 64 + xlo * 32, 32)]
        send(half, half, rgather.at[which, 15], sibling)

    def gather_finish(v, which):
        for i in range(8):
            arrived(at_block(v, 0, 0, 0), rgather.at[which, 7 + i])
        half = v.at[pl.ds(core * 64 + (1 - xlo) * 32, 32)]
        send(half, half, rgather.at[which, 16], sibling)
        arrived(half, rgather.at[which, 15])
        arrived(half, rgather.at[which, 16])

    def put_blocks(v, value):
        base = core * 64 + (xlo * 8 + z) * 4
        for b in range(4):
            v[base + b] = value[:, b * BLK : (b + 1) * BLK].astype(BF)

    def joined(ref):
        return ref[...].reshape(F, ROWS * BLK)

    def product(v):
        def step(q, totals):
            totals = list(totals)
            for r in range(ROWS):
                for s in range(0, MINE, 2):
                    b = q * 16 + r * MINE + s
                    k = q * MINE + s
                    left = jnp.concatenate([v[cols[r, k]], v[cols[r, k + 1]]], axis=1)
                    right = jnp.concatenate([vals[b], vals[b + 1]], axis=1)
                    totals[r] = totals[r] + nt(left, right)
            return tuple(totals)

        zero = jnp.zeros((WIDE, BLK), F32)
        return lax.fori_loop(0, 8, step, (zero,) * ROWS)

    def transposed(g, which):
        to_core, from_core, to_beside, from_beside, to_z, from_z = bufs[6 * which : 6 * which + 6]
        kept = red
        sems = rred.at[which]

        def term(half, xl, i):
            zz = (z + far_first(i)) % 8
            p = dom_at(xl, zz, half) * 4
            sums = []
            for b in range(0, 4, 2):
                total = None
                for r in range(0, ROWS, 2):
                    right = jnp.concatenate(
                        [
                            jnp.concatenate(
                                [vals[inv[r + e, p + b]], vals[inv[r + e, p + b + 1]]], axis=1
                            )
                            for e in range(2)
                        ],
                        axis=0,
                    )
                    got = jnp.dot(
                        g[:, r * BLK : (r + 2) * BLK], right, preferred_element_type=F32
                    )
                    total = got if total is None else total + got
                sums += [total[:, :BLK], total[:, BLK:]]
            return jnp.stack(sums)

        for group in range(4):
            xl = 1 - xlo if group < 2 else xlo

            def one(i, unused):
                to_core[group // 2 * 8 + i] = term(1 - core, xl, i).astype(BF)
                return unused

            at = group % 2 * 4
            lax.fori_loop(at, at + 4, one, 0)
            span = pl.ds(group * 4, 4)
            send(to_core.at[span], from_core.at[span], sems.at[group], sibling)
        for group in range(2):
            span = pl.ds(group * 4, 4)
            arrived(from_core.at[span], sems.at[group])

            def two(i, unused):
                total = term(core, 1 - xlo, i) + from_core[i].astype(F32)
                to_beside[i] = total.astype(BF)
                return unused

            lax.fori_loop(group * 4, group * 4 + 4, two, 0)
            send(to_beside.at[span], from_beside.at[span], sems.at[4 + group], beside)
        for group in range(2):
            arrived(from_core.at[pl.ds(8 + group * 4, 4)], sems.at[2 + group])

            def three(i, unused):
                kept[i] = term(core, xlo, i) + from_core[8 + i].astype(F32)
                return unused

            lax.fori_loop(group * 4, group * 4 + 4, three, 0)
        for group in range(2):
            arrived(from_beside.at[pl.ds(group * 4, 4)], sems.at[4 + group])
            for i in range(group * 4, group * 4 + 4):
                total = kept[i] + from_beside[i].astype(F32)
                if i < 7:
                    to_z[i] = total.astype(BF)
                    send(to_z.at[i], from_z.at[i], sems.at[6 + i], along(far_first(i)))
        for i in range(7):
            arrived(from_z.at[i], sems.at[6 + i])
            total = total + from_z[i].astype(F32)
        return jnp.concatenate([total[b] for b in range(4)], axis=1).astype(BF)

    zero_block = jnp.zeros((1, BLK, BLK), BF)
    vals[pl.ds(NBLK, 1)] = zero_block
    v1[pl.ds(NBLK, 1)] = zero_block[:, :WIDE]
    v2[pl.ds(NBLK, 1)] = zero_block[:, :WIDE]
    feats[c] = feats_in[...]
    collect(feats, 0)
    proj = jnp.dot(w1_cols[...], joined(feats), preferred_element_type=F32)
    put_blocks(v1, proj)
    gather_start(v1, 0)

    relay(0)
    relay(1)
    gather_relay(v1, 0)
    cross(0)
    relay(2)
    cross(1)
    relay(3)
    gather_finish(v1, 0)
    cross(2)
    cross(3)
    for r in range(ROWS):
        for q in (far_below, far_above, far_opposite):
            take(q, r)
    own.wait()

    for r, total in enumerate(product(v1)):
        first[:, r * BLK : (r + 1) * BLK] = total
    hidden = (first[...] * jax.nn.sigmoid(first[...])).astype(BF)
    hid[c] = hidden
    spread(hid.at[c], hid, 1)

    back_second = transposed(cot_in[...], 0)
    back[c] = back_second
    spread(back.at[c], back, 2)

    collect(hid, 1)
    put_blocks(v2, jnp.dot(w2_cols[...], joined(hid), preferred_element_type=F32))
    gather_start(v2, 1)

    collect(back, 2)
    hidden_grad = jnp.dot(w2_rows[...], joined(back), preferred_element_type=F32)
    value = first[...]
    sig = jax.nn.sigmoid(value)
    act_grad = (hidden_grad * (sig + value * sig * (1.0 - sig))).astype(BF)
    back_first = transposed(act_grad, 1)
    grad_second = nt(back[c], joined(hid))
    grad_first = nt(back_first, joined(feats))

    terms, quarters, along_z, whole = bufs[12:16]
    for n, grad in enumerate((grad_second, grad_first)):
        for k in range(4):
            terms[k, n] = grad[k * 8 : k * 8 + 8]
    me = xlo * 2 + core
    pair = [
        (beside, (1 - xlo) * 2 + core),
        (sibling, xlo * 2 + 1 - core),
        (corner, (1 - xlo) * 2 + 1 - core),
    ]
    for n, (to, k) in enumerate(pair):
        send(terms.at[k], quarters.at[n], rgrad.at[n], to)
    gather_relay(v2, 1)
    total = terms[me]
    for n in range(3):
        arrived(quarters.at[n], rgrad.at[n])
        total = total + quarters[n]
    along_z[7] = total
    for i in range(7):
        send(along_z.at[7], along_z.at[i], rgrad.at[3 + i], along(far_first(i)))
    gather_finish(v2, 1)
    for r, total in enumerate(product(v2)):
        out_ref[:, r * BLK : (r + 1) * BLK] = total
    total = along_z[7]
    for i in range(7):
        arrived(along_z.at[i], rgrad.at[3 + i])
        total = total + along_z[i]
    whole[me] = total
    for n, (to, k) in enumerate(pair):
        send(whole.at[me], whole.at[me], rgrad.at[10 + n], to)
    for n, (to, k) in enumerate(pair):
        arrived(whole.at[k], rgrad.at[10 + n])
    for k in range(4):
        for n in range(2):
            grads_ref[n, k * 8 : k * 8 + 8] = whole[k, n]
    for copy in started:
        copy.wait_send()


def body(feats, w_first, w_second, block_cols, block_count, block_vals, cotangent):
    c = lax.axis_index("col")
    slots = jnp.arange(block_cols.shape[1])
    used = slots[None, :] < block_count[:, None]
    b, core, rest = block_cols % 4, block_cols // 4 % 2, block_cols // 8
    cols = jnp.where(used, core * 64 + rest * 4 + b, NBLK).astype(jnp.int32)
    place = slots[None, :] // MINE * 16 + jnp.arange(ROWS)[:, None] * MINE + slots[None, :] % MINE
    hit = used[:, :, None] & (block_cols[:, :, None] == jnp.arange(NBLK)[None, None, :])
    inv = (NBLK + jnp.sum(jnp.where(hit, place[:, :, None] - NBLK, 0), axis=1)).astype(jnp.int32)
    w1_cols = lax.dynamic_slice_in_dim(w_first, c * WIDE, WIDE, 1).T
    w2_cols = lax.dynamic_slice_in_dim(w_second, c * WIDE, WIDE, 1).T
    w2_rows = lax.dynamic_slice_in_dim(w_second, c * WIDE, WIDE, 0)

    blocks = lambda n, kind: pltpu.VMEM((n, 4, WIDE, BLK), kind)
    reduce_bufs = [blocks(16, BF), blocks(16, BF), blocks(8, BF), blocks(8, BF), blocks(8, BF), blocks(8, BF)]
    grad_bufs = [pltpu.VMEM((n, 2, 8, F), F32) for n in (4, 3, 8, 4)]
    vmem = pl.BlockSpec(memory_space=pltpu.VMEM)
    smem = pl.BlockSpec(memory_space=pltpu.SMEM)
    wide = pltpu.VMEM((8, WIDE, ROWS * BLK), BF)
    out, grads = pl.pallas_call(
        kernel,
        out_shape=(
            jax.ShapeDtypeStruct((WIDE, ROWS * BLK), F32),
            jax.ShapeDtypeStruct((2, WIDE, F), F32),
        ),
        in_specs=[smem, smem] + [vmem] * 6,
        out_specs=(vmem, vmem),
        scratch_shapes=[
            pltpu.VMEM((NBLK + 1, BLK, BLK), BF),
            wide,
            wide,
            wide,
            pltpu.VMEM((WIDE, ROWS * BLK), F32),
            pltpu.VMEM((NBLK + 1, WIDE, BLK), BF),
            pltpu.VMEM((NBLK + 1, WIDE, BLK), BF),
            reduce_bufs * 2 + grad_bufs,
            blocks(8, F32),
            pltpu.SemaphoreType.DMA((160,)),
            pltpu.SemaphoreType.DMA((8, 4)),
            pltpu.SemaphoreType.DMA((3, 7)),
            pltpu.SemaphoreType.DMA((2, 17)),
            pltpu.SemaphoreType.DMA((2, 13)),
            pltpu.SemaphoreType.DMA((13,)),
            pltpu.SemaphoreType.DMA,
        ],
        compiler_params=pltpu.CompilerParams(
            collective_id=0, has_side_effects=True, vmem_limit_bytes=40 << 20
        ),
        name="graph_layers",
    )(
        cols,
        inv,
        feats.T,
        cotangent.T,
        w1_cols,
        w2_cols,
        w2_rows,
        block_vals.reshape(ROWS * MINE, BLK, BLK),
    )
    return (out.T, grads[1].T, grads[0].T)


def solution(mesh):
    return jax.shard_map(
        body,
        mesh=mesh,
        in_specs=(
            P("dom", "col"),
            P(),
            P(),
            P("dom", None),
            P("dom"),
            P("dom", "col", None, None),
            P("dom", "col"),
        ),
        out_specs=(P("dom", "col"), P(None, "col"), P(None, "col")),
        check_vma=False,
    )
```

```python
import functools

import jax
import jax.numpy as jnp
from jax import lax
from jax.experimental import pallas as pl
from jax.experimental.pallas import tpu as pltpu
from jax.sharding import PartitionSpec as P

BLK = 128
ROWS = 4
MINE = 4
NBLK = 128
WIDE = 32
F = 256
MESH = pl.DeviceIdType.MESH
BF = jnp.bfloat16
F32 = jnp.float32


def far_first(i):
    return 4 + ((i + 1) // 2) * (1 - 2 * (i % 2))


def nt(a, b):
    return lax.dot_general(a, b, (((1,), (1,)), ((), ())), preferred_element_type=F32)


def kernel(
    feats_in,
    cot_in,
    w1_in,
    w2_in,
    vals_in,
    cols_in,
    count_in,
    out_ref,
    grads_ref,
    vals,
    feats,
    hid,
    back,
    first,
    v1,
    v2,
    w1,
    w2,
    w1_t,
    w2_t,
    cot,
    inv_rows,
    cols,
    count,
    inv,
    bufs,
    red,
    ssem,
    rvals,
    rcol,
    rgather,
    rred,
    rgrad,
    lsem,
    news,
):
    d, c = lax.axis_index("dom"), lax.axis_index("col")
    xlo, z, core = d // 16, (d // 2) % 8, d % 2
    xhi, y = c // 4, c % 4

    def dom_at(xl, zz, cc):
        return (xl * 8 + zz) * 2 + cc

    def col_at(xh, yy):
        return xh * 4 + yy % 4

    up, down = (d, col_at(xhi, y + 1)), (d, col_at(xhi, y + 3))
    across = (d, col_at(1 - xhi, y))
    beside = (dom_at(1 - xlo, z, core), c)
    sibling = (dom_at(xlo, z, 1 - core), c)
    corner = (dom_at(1 - xlo, z, 1 - core), c)

    def along(k):
        return (dom_at(xlo, (z + k) % 8, core), c)

    col_peers = [
        (d, col_at((xhi + a) % 2, y + b)) for a in range(2) for b in range(4) if a + b
    ]

    started = []

    def send(src, dst, sem, to):
        copy = pltpu.make_async_remote_copy(
            src_ref=src,
            dst_ref=dst,
            send_sem=ssem.at[len(started)],
            recv_sem=sem,
            device_id=to,
            device_id_type=MESH,
        )
        copy.start()
        started.append(copy)

    def arrived(dst, sem):
        pltpu.make_async_remote_copy(
            src_ref=dst,
            dst_ref=dst,
            send_sem=ssem.at[0],
            recv_sem=sem,
            device_id=up,
            device_id_type=MESH,
        ).wait_recv()

    def local(src, dst, n):
        copy = pltpu.make_async_copy(src, dst, lsem.at[n])
        copy.start()
        return copy

    near = [up, down, across, beside, sibling, corner, along(1), along(7)]
    barrier = pltpu.get_barrier_semaphore()
    for peer in near:
        pl.semaphore_signal(barrier, inc=1, device_id=peer, device_id_type=MESH)
    loads = [
        local(cols_in, cols, 0),
        local(count_in, count, 1),
        local(feats_in, feats.at[c], 2),
        local(w1_in, w1, 3),
        local(w2_in, w2, 4),
        local(cot_in, cot, 5),
        local(vals_in, vals.at[pl.ds(c * 16, 16)], 6),
    ]
    pl.semaphore_wait(barrier, len(near))

    for k in (1, 7):
        pl.semaphore_signal(news.at[0], inc=1, device_id=along(k), device_id_type=MESH)

    def hear_far():
        pl.semaphore_wait(news.at[0], 2)
        for k in (2, 6):
            pl.semaphore_signal(news.at[1], inc=1, device_id=along(k), device_id_type=MESH)

    def spread(src, full, which):
        for n, peer in enumerate(col_peers):
            send(src, full.at[c], rcol.at[which, n], peer)

    def collect(full, which):
        for n in range(7):
            arrived(full.at[0], rcol.at[which, n])

    def part(q, r):
        return feats.at[q] if r == ROWS else vals.at[pl.ds(q * 16 + r * MINE, MINE)]

    def send_own(r, to):
        src = feats_in if r == ROWS else vals_in.at[pl.ds(r * MINE, MINE)]
        send(src, part(c, r), rvals.at[c, r], to)

    for r in (ROWS, 0, 1, 2, 3):
        send_own(r, up)
        send_own((2, 3, 0, 1, ROWS)[r], down)
        send_own(r, across)

    below, above = col_at(xhi, y + 3), col_at(xhi, y + 1)
    partner, opposite = col_at(1 - xhi, y), col_at(xhi, y + 2)
    far_below, far_above = col_at(1 - xhi, y + 3), col_at(1 - xhi, y + 1)
    far_opposite = col_at(1 - xhi, y + 2)

    def take(q, r):
        arrived(part(q, r), rvals.at[q, r])

    def pass_on(q, r, to):
        send(part(q, r), part(q, r), rvals.at[q, r], to)

    def forward(q, r, to):
        take(q, r)
        if to is not None:
            pass_on(q, r, to)

    def both_ways(r):
        take(partner, r)
        pass_on(partner, r, up)
        pass_on(partner, r, down)

    def at_block(v, xl, zz, cc):
        return v.at[pl.ds(cc * 64 + (xl * 8 + zz) * 4, 4)]

    def gather_start(v, which):
        mine = at_block(v, xlo, z, core)
        send(mine, mine, rgather.at[which, 14], beside)
        for i in range(7):
            send(mine, mine, rgather.at[which, i], along(far_first(i)))

    def gather_second(v, which):
        other = at_block(v, 1 - xlo, z, core)
        arrived(other, rgather.at[which, 14])
        for i in range(7):
            send(other, other, rgather.at[which, 7 + i], along(far_first(i)))

    def gather_share(v, which):
        for i in range(14):
            arrived(at_block(v, 0, 0, 0), rgather.at[which, i])
        half = v.at[pl.ds(core * 64, 64)]
        send(half, half, rgather.at[which, 15], sibling)

    def gather_finish(v, which):
        arrived(v.at[pl.ds(0, 64)], rgather.at[which, 15])

    def put_blocks(v, value):
        base = core * 64 + (xlo * 8 + z) * 4
        for b in range(4):
            v[base + b] = value[:, b * BLK : (b + 1) * BLK].astype(BF)

    def joined(ref):
        return ref[...].reshape(F, ROWS * BLK)

    def block_of(r, k):
        p = cols[r, k]
        return jnp.where(k < count[r], p // 4 % 2 * 64 + p // 8 * 4 + p % 4, NBLK)

    def product(v, rows):
        def step(q, totals):
            totals = list(totals)
            for n, r in enumerate(rows):
                for s in range(0, MINE, 2):
                    b = q * 16 + r * MINE + s
                    k = q * MINE + s
                    left = jnp.concatenate([v[block_of(r, k)], v[block_of(r, k + 1)]], axis=1)
                    right = jnp.concatenate([vals[b], vals[b + 1]], axis=1)
                    totals[n] = totals[n] + nt(left, right)
            return tuple(totals)

        zero = jnp.zeros((WIDE, BLK), F32)
        return lax.fori_loop(0, 8, step, (zero,) * len(rows), unroll=4)

    def transposed(g, which, meanwhile):
        to_core, from_core, to_beside, from_beside, to_z, from_z = bufs[6 * which : 6 * which + 6]
        kept = red
        sems = rred.at[which]

        def term(half, xl, i):
            zz = (z + far_first(i)) % 8
            p = dom_at(xl, zz, half) * 4
            sums = []
            for b in range(0, 4, 2):
                total = None
                for r in range(0, ROWS, 2):
                    right = jnp.concatenate(
                        [
                            jnp.concatenate(
                                [vals[inv[r + e, p + b]], vals[inv[r + e, p + b + 1]]], axis=1
                            )
                            for e in range(2)
                        ],
                        axis=0,
                    )
                    got = jnp.dot(
                        g[:, r * BLK : (r + 2) * BLK], right, preferred_element_type=F32
                    )
                    total = got if total is None else total + got
                sums += [total[:, :BLK], total[:, BLK:]]
            return jnp.stack(sums)

        def over(at, n, write):
            def one(i, unused):
                write(i)
                return unused

            lax.fori_loop(at, at + n, one, 0, unroll=n)

        for group in range(4):
            xl = 1 - xlo if group < 2 else xlo

            def one(i):
                to_core[group // 2 * 8 + i] = term(1 - core, xl, i).astype(BF)

            over(group % 2 * 4, 4, one)
            span = pl.ds(group * 4, 4)
            send(to_core.at[span], from_core.at[span], sems.at[group], sibling)
        for group in range(4):
            if group % 2 == 0:
                arrived(from_core.at[pl.ds(group * 2, 4)], sems.at[group // 2])

            def two(i):
                total = term(core, 1 - xlo, i) + from_core[i].astype(F32)
                to_beside[i] = total.astype(BF)

            over(group * 2, 2, two)
            span = pl.ds(group * 2, 2)
            send(to_beside.at[span], from_beside.at[span], sems.at[4 + group], beside)
        for group in range(2):
            arrived(from_core.at[pl.ds(8 + group * 4, 4)], sems.at[2 + group])

            def three(i):
                kept[i] = term(core, xlo, i) + from_core[8 + i].astype(F32)

            over(group * 4, 4, three)
        meanwhile[0]()
        for group in range(4):
            arrived(from_beside.at[pl.ds(group * 2, 2)], sems.at[4 + group])
            for i in range(group * 2, group * 2 + 2):
                total = kept[i] + from_beside[i].astype(F32)
                if i < 7:
                    to_z[i] = total.astype(BF)
                    send(to_z.at[i], from_z.at[i], sems.at[8 + i], along(far_first(i)))
        kept[7] = total
        meanwhile[1]()
        total = kept[7]
        for i in range(7):
            arrived(from_z.at[i], sems.at[8 + i])
            total = total + from_z[i].astype(F32)
        return jnp.concatenate([total[b] for b in range(4)], axis=1).astype(BF)

    zero_block = jnp.zeros((1, BLK, BLK), BF)
    vals[pl.ds(NBLK, 1)] = zero_block
    v1[pl.ds(NBLK, 1)] = zero_block[:, :WIDE]
    v2[pl.ds(NBLK, 1)] = zero_block[:, :WIDE]
    hear_far()
    for copy in loads:
        copy.wait()
    lane = lax.broadcasted_iota(jnp.int32, (1, NBLK), 1)
    for r in range(ROWS):

        def mark(k, found):
            place = k // MINE * 16 + r * MINE + k % MINE - NBLK
            return found + jnp.where((lane == cols[r, k]) & (k < count[r]), place, 0)

        empty = jnp.full((1, NBLK), NBLK, jnp.int32)
        inv_rows[r : r + 1] = lax.fori_loop(0, 32, mark, empty, unroll=8)
    to_scalars = local(inv_rows, inv, 0)
    forward(below, ROWS, up)
    forward(above, ROWS, None)
    both_ways(ROWS)
    w1_t[...] = w1[...].T
    forward(below, 0, up)
    forward(above, 2, down)
    w2_t[...] = w2[...].T
    forward(opposite, ROWS, across)
    for q in (far_below, far_above, far_opposite):
        take(q, ROWS)
    pl.semaphore_wait(news.at[1], 2)
    mine = pl.ds(c * WIDE, WIDE)
    put_blocks(v1, jnp.dot(w1_t[mine, :], joined(feats), preferred_element_type=F32))
    gather_start(v1, 0)

    both_ways(0)
    forward(below, 1, up)
    forward(above, 3, down)
    forward(opposite, 0, across)
    forward(opposite, 2, across)
    gather_second(v1, 0)
    both_ways(1)
    forward(opposite, 1, across)
    forward(opposite, 3, across)
    both_ways(2)
    both_ways(3)
    gather_share(v1, 0)
    for q, rows in ((below, (2, 3)), (above, (0, 1))):
        for r in rows:
            take(q, r)
    to_scalars.wait()
    for r in range(ROWS):
        for q in (far_below, far_above, far_opposite):
            take(q, r)
    gather_finish(v1, 0)

    def layer_rows(rows):
        for r, total in zip(rows, product(v1, rows)):
            first[:, r * BLK : (r + 1) * BLK] = total

    def after_first():
        layer_rows((2, 3))
        hidden = (first[...] * jax.nn.sigmoid(first[...])).astype(BF)
        hid[c] = hidden
        spread(hid.at[c], hid, 1)

    back_second = transposed(cot[...], 0, (lambda: layer_rows((0, 1)), after_first))
    back[c] = back_second
    spread(back.at[c], back, 2)

    collect(hid, 1)
    put_blocks(v2, jnp.dot(w2_t[mine, :], joined(hid), preferred_element_type=F32))
    gather_start(v2, 1)
    gather_second(v2, 1)

    collect(back, 2)
    hidden_grad = jnp.dot(w2[mine, :], joined(back), preferred_element_type=F32)
    value = first[...]
    sig = jax.nn.sigmoid(value)
    act_grad = (hidden_grad * (sig + value * sig * (1.0 - sig))).astype(BF)
    back_first = transposed(
        act_grad, 1, (lambda: None, lambda: gather_share(v2, 1))
    )
    grad_second = nt(back[c], joined(hid))
    grad_first = nt(back_first, joined(feats))

    terms, quarters, along_z, whole = bufs[12:16]
    for n, grad in enumerate((grad_second, grad_first)):
        for k in range(4):
            terms[k, n] = grad[k * 8 : k * 8 + 8]
    me = xlo * 2 + core
    pair = [
        (beside, (1 - xlo) * 2 + core),
        (sibling, xlo * 2 + 1 - core),
        (corner, (1 - xlo) * 2 + 1 - core),
    ]
    for n, (to, k) in enumerate(pair):
        send(terms.at[k], quarters.at[n], rgrad.at[n], to)
    total = terms[me]
    for n in range(3):
        arrived(quarters.at[n], rgrad.at[n])
        total = total + quarters[n]
    along_z[7] = total
    for i in range(7):
        send(along_z.at[7], along_z.at[i], rgrad.at[3 + i], along(far_first(i)))
    gather_finish(v2, 1)
    for r, total in enumerate(product(v2, range(ROWS))):
        out_ref[:, r * BLK : (r + 1) * BLK] = total
    total = along_z[7]
    for i in range(7):
        arrived(along_z.at[i], rgrad.at[3 + i])
        total = total + along_z[i]
    whole[me] = total
    for n, (to, k) in enumerate(pair):
        send(whole.at[me], whole.at[me], rgrad.at[10 + n], to)
    for n, (to, k) in enumerate(pair):
        arrived(whole.at[k], rgrad.at[10 + n])
    for k in range(4):
        for n in range(2):
            grads_ref[n, k * 8 : k * 8 + 8] = whole[k, n]
    for copy in started:
        copy.wait_send()


def body(feats, w_first, w_second, block_cols, block_count, block_vals, cotangent):
    def blocks(n, kind):
        return pltpu.VMEM((n, 4, WIDE, BLK), kind)

    reduce_bufs = [blocks(n, BF) for n in (16, 16, 8, 8, 8, 8)]
    grad_bufs = [pltpu.VMEM((n, 2, 8, F), F32) for n in (4, 3, 8, 4)]
    vmem = pl.BlockSpec(memory_space=pltpu.VMEM)
    anywhere = pl.BlockSpec(memory_space=pl.ANY)
    wide = pltpu.VMEM((8, WIDE, ROWS * BLK), BF)
    square = pltpu.VMEM((F, F), BF)
    dma = pltpu.SemaphoreType.DMA
    out, grads = pl.pallas_call(
        kernel,
        out_shape=(
            jax.ShapeDtypeStruct((WIDE, ROWS * BLK), F32),
            jax.ShapeDtypeStruct((2, WIDE, F), F32),
        ),
        in_specs=[anywhere] * 7,
        out_specs=(vmem, vmem),
        scratch_shapes=[
            pltpu.VMEM((NBLK + 1, BLK, BLK), BF),
            wide,
            wide,
            wide,
            pltpu.VMEM((WIDE, ROWS * BLK), F32),
            pltpu.VMEM((NBLK + 1, WIDE, BLK), BF),
            pltpu.VMEM((NBLK + 1, WIDE, BLK), BF),
            square,
            square,
            square,
            square,
            pltpu.VMEM((WIDE, ROWS * BLK), BF),
            pltpu.VMEM((ROWS, NBLK), jnp.int32),
            pltpu.SMEM((ROWS, 32), jnp.int32),
            pltpu.SMEM((ROWS,), jnp.int32),
            pltpu.SMEM((ROWS, NBLK), jnp.int32),
            reduce_bufs * 2 + grad_bufs,
            blocks(8, F32),
            dma((160,)),
            dma((8, 5)),
            dma((3, 7)),
            dma((2, 16)),
            dma((2, 15)),
            dma((13,)),
            dma((7,)),
            pltpu.SemaphoreType.REGULAR((2,)),
        ],
        compiler_params=pltpu.CompilerParams(
            collective_id=0, has_side_effects=True, vmem_limit_bytes=56 << 20
        ),
        name="graph_layers",
    )(
        feats.T,
        cotangent.T,
        w_first,
        w_second,
        block_vals.reshape(ROWS * MINE, BLK, BLK),
        block_cols,
        block_count,
    )
    return (out.T, grads[1].T, grads[0].T)


def solution(mesh):
    return jax.shard_map(
        body,
        mesh=mesh,
        in_specs=(
            P("dom", "col"),
            P(),
            P(),
            P("dom", None),
            P("dom"),
            P("dom", "col", None, None),
            P("dom", "col"),
        ),
        out_specs=(P("dom", "col"), P(None, "col"), P(None, "col")),
        check_vma=False,
    )
```

```python
import functools

import jax
import jax.numpy as jnp
from jax import lax
from jax.experimental import pallas as pl
from jax.experimental.pallas import tpu as pltpu
from jax.sharding import PartitionSpec as P

BLK = 128
ROWS = 4
MINE = 4
NBLK = 128
WIDE = 32
F = 256
MESH = pl.DeviceIdType.MESH
BF = jnp.bfloat16
F32 = jnp.float32


def far_first(i):
    return 4 + ((i + 1) // 2) * (1 - 2 * (i % 2))


def nt(a, b):
    return lax.dot_general(a, b, (((1,), (1,)), ((), ())), preferred_element_type=F32)


def kernel(
    feats_in,
    cot_in,
    w1_in,
    w2_in,
    vals_in,
    cols_in,
    count_in,
    out_ref,
    grads_ref,
    vals,
    feats,
    agg,
    hid,
    back,
    first,
    v1,
    v2,
    w1,
    w2,
    w1_t,
    w2_t,
    cot,
    inv_rows,
    cols,
    count,
    inv,
    bufs,
    gbufs,
    ssem,
    rvals,
    rcol,
    rgather,
    rred,
    rgrad,
    lsem,
    news,
):
    d, c = lax.axis_index("dom"), lax.axis_index("col")
    xlo, z, core = d // 16, (d // 2) % 8, d % 2
    xhi, y = c // 4, c % 4

    def dom_at(xl, zz, cc):
        return (xl * 8 + zz) * 2 + cc

    def col_at(xh, yy):
        return xh * 4 + yy % 4

    up, down = (d, col_at(xhi, y + 1)), (d, col_at(xhi, y + 3))
    across = (d, col_at(1 - xhi, y))
    beside = (dom_at(1 - xlo, z, core), c)
    sibling = (dom_at(xlo, z, 1 - core), c)
    corner = (dom_at(1 - xlo, z, 1 - core), c)

    def along(k):
        return (dom_at(xlo, (z + k) % 8, core), c)

    col_peers = [
        (d, col_at((xhi + a) % 2, y + b)) for a in range(2) for b in range(4) if a + b
    ]

    started = []

    def send(src, dst, sem, to):
        copy = pltpu.make_async_remote_copy(
            src_ref=src,
            dst_ref=dst,
            send_sem=ssem.at[len(started)],
            recv_sem=sem,
            device_id=to,
            device_id_type=MESH,
        )
        copy.start()
        started.append(copy)

    def arrived(dst, sem):
        pltpu.make_async_remote_copy(
            src_ref=dst,
            dst_ref=dst,
            send_sem=ssem.at[0],
            recv_sem=sem,
            device_id=up,
            device_id_type=MESH,
        ).wait_recv()

    def local(src, dst, n):
        copy = pltpu.make_async_copy(src, dst, lsem.at[n])
        copy.start()
        return copy

    near = [up, down, across, beside, sibling, corner, along(1), along(7)]
    barrier = pltpu.get_barrier_semaphore()
    for peer in near:
        pl.semaphore_signal(barrier, inc=1, device_id=peer, device_id_type=MESH)
    loads = [
        local(cols_in, cols, 0),
        local(count_in, count, 1),
        local(w1_in, w1, 3),
        local(w2_in, w2, 4),
        local(feats_in, feats, 2),
        local(cot_in, cot, 5),
        local(vals_in, vals.at[pl.ds(c * 16, 16)], 6),
    ]
    pl.semaphore_wait(barrier, len(near))

    for k in (1, 7):
        pl.semaphore_signal(news.at[0], inc=1, device_id=along(k), device_id_type=MESH)

    def hear_far():
        pl.semaphore_wait(news.at[0], 2)
        for k in (2, 6):
            pl.semaphore_signal(news.at[1], inc=1, device_id=along(k), device_id_type=MESH)

    def spread(src, full, which):
        for n, peer in enumerate(col_peers):
            send(src, full.at[c], rcol.at[which, n], peer)

    def collect(full, which):
        for n in range(7):
            arrived(full.at[0], rcol.at[which, n])

    def part(q, r):
        return vals.at[pl.ds(q * 16 + r * MINE, MINE)]

    def send_own(r, to):
        send(vals_in.at[pl.ds(r * MINE, MINE)], part(c, r), rvals.at[c, r], to)

    for r in range(ROWS):
        send_own(r, up)
        send_own((2, 3, 0, 1)[r], down)
        send_own(r, across)

    below, above = col_at(xhi, y + 3), col_at(xhi, y + 1)
    partner, opposite = col_at(1 - xhi, y), col_at(xhi, y + 2)
    far_below, far_above = col_at(1 - xhi, y + 3), col_at(1 - xhi, y + 1)
    far_opposite = col_at(1 - xhi, y + 2)

    def take(q, r):
        arrived(part(q, r), rvals.at[q, r])

    def pass_on(q, r, to):
        send(part(q, r), part(q, r), rvals.at[q, r], to)

    def forward(q, r, to):
        take(q, r)
        if to is not None:
            pass_on(q, r, to)

    def both_ways(r):
        take(partner, r)
        pass_on(partner, r, up)
        pass_on(partner, r, down)

    def at_block(v, xl, zz, cc):
        return v.at[pl.ds(cc * 64 + (xl * 8 + zz) * 4, 4)]

    def gather_start(v, which):
        mine = at_block(v, xlo, z, core)
        send(mine, mine, rgather.at[which, 14], beside)
        for i in range(7):
            send(mine, mine, rgather.at[which, i], along(far_first(i)))

    def gather_second(v, which):
        other = at_block(v, 1 - xlo, z, core)
        arrived(other, rgather.at[which, 14])
        for i in range(7):
            send(other, other, rgather.at[which, 7 + i], along(far_first(i)))

    def gather_share(v, which):
        for i in range(14):
            arrived(at_block(v, 0, 0, 0), rgather.at[which, i])
        half = v.at[pl.ds(core * 64, 64)]
        send(half, half, rgather.at[which, 15], sibling)

    def gather_finish(v, which):
        arrived(v.at[pl.ds(0, 64)], rgather.at[which, 15])

    def put_blocks(v, value):
        base = core * 64 + (xlo * 8 + z) * 4
        for b in range(4):
            v[base + b] = value[:, b * BLK : (b + 1) * BLK].astype(BF)

    def joined(ref):
        return ref[...].reshape(F, ROWS * BLK)

    def block_of(r, k):
        p = cols[r, k]
        return jnp.where(k < count[r], p // 4 % 2 * 64 + p // 8 * 4 + p % 4, NBLK)

    def product(v, rows):
        def step(q, totals):
            totals = list(totals)
            for n, r in enumerate(rows):
                for s in range(0, MINE, 2):
                    b = q * 16 + r * MINE + s
                    k = q * MINE + s
                    left = jnp.concatenate([v[block_of(r, k)], v[block_of(r, k + 1)]], axis=1)
                    right = jnp.concatenate([vals[b], vals[b + 1]], axis=1)
                    totals[n] = totals[n] + nt(left, right)
            return tuple(totals)

        zero = jnp.zeros((WIDE, BLK), F32)
        return lax.fori_loop(0, 8, step, (zero,) * len(rows), unroll=4)

    def transposed(g, meanwhile):
        to_core, from_core, to_beside, from_beside, to_z, from_z, kept = bufs
        sems = rred

        def term(half, xl, i):
            zz = (z + far_first(i)) % 8
            p = dom_at(xl, zz, half) * 4
            sums = []
            for b in range(0, 4, 2):
                total = None
                for r in range(0, ROWS, 2):
                    right = jnp.concatenate(
                        [
                            jnp.concatenate(
                                [vals[inv[r + e, p + b]], vals[inv[r + e, p + b + 1]]], axis=1
                            )
                            for e in range(2)
                        ],
                        axis=0,
                    )
                    got = jnp.dot(
                        g[:, r * BLK : (r + 2) * BLK], right, preferred_element_type=F32
                    )
                    total = got if total is None else total + got
                sums += [total[:, :BLK], total[:, BLK:]]
            return jnp.stack(sums)

        def over(at, n, write):
            def one(i, unused):
                write(i)
                return unused

            lax.fori_loop(at, at + n, one, 0, unroll=n)

        for group in range(4):
            xl = 1 - xlo if group < 2 else xlo

            def one(i):
                to_core[group // 2 * 8 + i] = term(1 - core, xl, i).astype(BF)

            over(group % 2 * 4, 4, one)
            span = pl.ds(group * 4, 4)
            send(to_core.at[span], from_core.at[span], sems.at[group], sibling)
        for group in range(4):
            if group % 2 == 0:
                arrived(from_core.at[pl.ds(group * 2, 4)], sems.at[group // 2])

            def two(i):
                total = term(core, 1 - xlo, i) + from_core[i].astype(F32)
                to_beside[i] = total.astype(BF)

            over(group * 2, 2, two)
            span = pl.ds(group * 2, 2)
            send(to_beside.at[span], from_beside.at[span], sems.at[4 + group], beside)
        for group in range(2):
            arrived(from_core.at[pl.ds(8 + group * 4, 4)], sems.at[2 + group])

            def three(i):
                kept[i] = term(core, xlo, i) + from_core[8 + i].astype(F32)

            over(group * 4, 4, three)
        meanwhile[0]()
        for group in range(4):
            arrived(from_beside.at[pl.ds(group * 2, 2)], sems.at[4 + group])
            for i in range(group * 2, group * 2 + 2):
                total = kept[i] + from_beside[i].astype(F32)
                if i < 7:
                    to_z[i] = total.astype(BF)
                    send(to_z.at[i], from_z.at[i], sems.at[8 + i], along(far_first(i)))
        kept[7] = total
        meanwhile[1]()
        total = kept[7]
        for i in range(7):
            arrived(from_z.at[i], sems.at[8 + i])
            total = total + from_z[i].astype(F32)
        return jnp.concatenate([total[b] for b in range(4)], axis=1).astype(BF)

    zero_block = jnp.zeros((1, BLK, BLK), BF)
    vals[pl.ds(NBLK, 1)] = zero_block
    v1[pl.ds(NBLK, 1)] = zero_block[:, :WIDE]
    v2[pl.ds(NBLK, 1)] = zero_block[:, :WIDE]
    hear_far()
    for copy in loads:
        copy.wait()
    put_blocks(v1, feats[...])
    pl.semaphore_wait(news.at[1], 2)
    gather_start(v1, 0)
    lane = lax.broadcasted_iota(jnp.int32, (1, NBLK), 1)
    for r in range(ROWS):

        def mark(k, found):
            place = k // MINE * 16 + r * MINE + k % MINE - NBLK
            return found + jnp.where((lane == cols[r, k]) & (k < count[r]), place, 0)

        empty = jnp.full((1, NBLK), NBLK, jnp.int32)
        inv_rows[r : r + 1] = lax.fori_loop(0, 32, mark, empty, unroll=8)
    to_scalars = local(inv_rows, inv, 0)
    forward(below, 0, up)
    forward(above, 2, down)
    gather_second(v1, 0)
    both_ways(0)
    forward(below, 1, up)
    forward(above, 3, down)
    forward(opposite, 0, across)
    forward(opposite, 2, across)
    w1_t[...] = w1[...].T
    w2_t[...] = w2[...].T
    both_ways(1)
    forward(opposite, 1, across)
    forward(opposite, 3, across)
    both_ways(2)
    gather_share(v1, 0)
    both_ways(3)
    for q, rows in ((below, (2, 3)), (above, (0, 1))):
        for r in rows:
            take(q, r)
    to_scalars.wait()
    for r in range(ROWS):
        for q in (far_below, far_above, far_opposite):
            take(q, r)
    gather_finish(v1, 0)

    for r, total in enumerate(product(v1, range(ROWS))):
        agg[c, :, r * BLK : (r + 1) * BLK] = total.astype(BF)
    spread(agg.at[c], agg, 0)
    mine = pl.ds(c * WIDE, WIDE)

    def after_agg():
        collect(agg, 0)
        value = jnp.dot(w1_t[mine, :], joined(agg), preferred_element_type=F32)
        first[...] = value
        hid[c] = (value * jax.nn.sigmoid(value)).astype(BF)
        spread(hid.at[c], hid, 1)

    def after_hidden():
        collect(hid, 1)
        put_blocks(v2, jnp.dot(w2_t[mine, :], joined(hid), preferred_element_type=F32))
        gather_start(v2, 1)

    back[c] = transposed(cot[...], (after_agg, after_hidden))
    spread(back.at[c], back, 2)
    gather_second(v2, 1)

    me = xlo * 2 + core
    pair = [
        (beside, (1 - xlo) * 2 + core),
        (sibling, xlo * 2 + 1 - core),
        (corner, (1 - xlo) * 2 + 1 - core),
    ]

    def quarters_out(n, grad):
        terms, quarters, along_z, whole = gbufs[n]
        for k in range(4):
            terms[k] = grad[k * 8 : k * 8 + 8]
        for i, (to, k) in enumerate(pair):
            send(terms.at[k], quarters.at[i], rgrad.at[n, i], to)

    def sums_out(n):
        terms, quarters, along_z, whole = gbufs[n]
        total = terms[me]
        for i in range(3):
            arrived(quarters.at[i], rgrad.at[n, i])
            total = total + quarters[i]
        along_z[7] = total
        for i in range(7):
            send(along_z.at[7], along_z.at[i], rgrad.at[n, 3 + i], along(far_first(i)))

    def totals_out(n):
        terms, quarters, along_z, whole = gbufs[n]
        total = along_z[7]
        for i in range(7):
            arrived(along_z.at[i], rgrad.at[n, 3 + i])
            total = total + along_z[i]
        whole[me] = total
        for i, (to, k) in enumerate(pair):
            send(whole.at[me], whole.at[me], rgrad.at[n, 10 + i], to)

    def totals_in(n):
        terms, quarters, along_z, whole = gbufs[n]
        for i, (to, k) in enumerate(pair):
            arrived(whole.at[k], rgrad.at[n, 10 + i])
        for k in range(4):
            grads_ref[n, k * 8 : k * 8 + 8] = whole[k]

    quarters_out(0, nt(back[c], joined(hid)))
    collect(back, 2)
    hidden_grad = jnp.dot(w2[mine, :], joined(back), preferred_element_type=F32)
    value = first[...]
    sig = jax.nn.sigmoid(value)
    act_grad = (hidden_grad * (sig + value * sig * (1.0 - sig))).astype(BF)
    quarters_out(1, nt(act_grad, joined(agg)))
    sums_out(0)
    sums_out(1)
    gather_share(v2, 1)
    totals_out(0)
    totals_out(1)

    gather_finish(v2, 1)
    for r, total in enumerate(product(v2, range(ROWS))):
        out_ref[:, r * BLK : (r + 1) * BLK] = total
    totals_in(0)
    totals_in(1)
    for copy in started:
        copy.wait_send()


def body(feats, w_first, w_second, block_cols, block_count, block_vals, cotangent):
    def blocks(n, kind):
        return pltpu.VMEM((n, 4, WIDE, BLK), kind)

    reduce_bufs = [blocks(n, BF) for n in (16, 16, 8, 8, 8, 8)]
    grad_bufs = [[pltpu.VMEM((n, 8, F), F32) for n in (4, 3, 8, 4)] for unused in range(2)]
    vmem = pl.BlockSpec(memory_space=pltpu.VMEM)
    anywhere = pl.BlockSpec(memory_space=pl.ANY)
    wide = pltpu.VMEM((8, WIDE, ROWS * BLK), BF)
    square = pltpu.VMEM((F, F), BF)
    dma = pltpu.SemaphoreType.DMA
    out, grads = pl.pallas_call(
        kernel,
        out_shape=(
            jax.ShapeDtypeStruct((WIDE, ROWS * BLK), F32),
            jax.ShapeDtypeStruct((2, WIDE, F), F32),
        ),
        in_specs=[anywhere] * 7,
        out_specs=(vmem, vmem),
        scratch_shapes=[
            pltpu.VMEM((NBLK + 1, BLK, BLK), BF),
            pltpu.VMEM((WIDE, ROWS * BLK), BF),
            wide,
            wide,
            wide,
            pltpu.VMEM((WIDE, ROWS * BLK), F32),
            pltpu.VMEM((NBLK + 1, WIDE, BLK), BF),
            pltpu.VMEM((NBLK + 1, WIDE, BLK), BF),
            square,
            square,
            square,
            square,
            pltpu.VMEM((WIDE, ROWS * BLK), BF),
            pltpu.VMEM((ROWS, NBLK), jnp.int32),
            pltpu.SMEM((ROWS, 32), jnp.int32),
            pltpu.SMEM((ROWS,), jnp.int32),
            pltpu.SMEM((ROWS, NBLK), jnp.int32),
            reduce_bufs + [blocks(8, F32)],
            grad_bufs,
            dma((160,)),
            dma((8, 4)),
            dma((3, 7)),
            dma((2, 16)),
            dma((15,)),
            dma((2, 13)),
            dma((7,)),
            pltpu.SemaphoreType.REGULAR((2,)),
        ],
        compiler_params=pltpu.CompilerParams(
            collective_id=0, has_side_effects=True, vmem_limit_bytes=56 << 20
        ),
        name="graph_layers",
    )(
        feats.T,
        cotangent.T,
        w_first,
        w_second,
        block_vals.reshape(ROWS * MINE, BLK, BLK),
        block_cols,
        block_count,
    )
    return (out.T, grads[1].T, grads[0].T)


def solution(mesh):
    return jax.shard_map(
        body,
        mesh=mesh,
        in_specs=(
            P("dom", "col"),
            P(),
            P(),
            P("dom", None),
            P("dom"),
            P("dom", "col", None, None),
            P("dom", "col"),
        ),
        out_specs=(P("dom", "col"), P(None, "col"), P(None, "col")),
        check_vma=False,
    )
```

```python
import functools

import jax
import jax.numpy as jnp
from jax import lax
from jax.experimental import pallas as pl
from jax.experimental.pallas import tpu as pltpu
from jax.sharding import PartitionSpec as P

BLK = 128
ROWS = 4
MINE = 4
NBLK = 128
MEANWHILE = 4
WIDE = 32
F = 256
MESH = pl.DeviceIdType.MESH
BF = jnp.bfloat16
F32 = jnp.float32


def far_first(i):
    return 4 + ((i + 1) // 2) * (1 - 2 * (i % 2))


def nt(a, b):
    return lax.dot_general(a, b, (((1,), (1,)), ((), ())), preferred_element_type=F32)


def kernel(
    feats_in,
    cot_in,
    w1_in,
    w2_in,
    vals_in,
    cols_in,
    count_in,
    out_ref,
    grads_ref,
    vals,
    feats,
    agg,
    hid,
    back,
    first,
    v1,
    v2,
    w1,
    w2,
    w1_t,
    w2_t,
    cot,
    inv_rows,
    cols,
    count,
    inv,
    bufs,
    gbufs,
    ssem,
    rvals,
    rcol,
    rgather,
    rred,
    rgrad,
    lsem,
    rhalf,
    news,
):
    d, c = lax.axis_index("dom"), lax.axis_index("col")
    xlo, z, core = d // 16, (d // 2) % 8, d % 2
    xhi, y = c // 4, c % 4

    def dom_at(xl, zz, cc):
        return (xl * 8 + zz) * 2 + cc

    def col_at(xh, yy):
        return xh * 4 + yy % 4

    up, down = (d, col_at(xhi, y + 1)), (d, col_at(xhi, y + 3))
    across = (d, col_at(1 - xhi, y))
    beside = (dom_at(1 - xlo, z, core), c)
    sibling = (dom_at(xlo, z, 1 - core), c)
    corner = (dom_at(1 - xlo, z, 1 - core), c)

    def along(k):
        return (dom_at(xlo, (z + k) % 8, core), c)

    col_peers = [
        (d, col_at((xhi + a) % 2, y + b)) for a in range(2) for b in range(4) if a + b
    ]

    def send(src, dst, sem, to, group):
        pltpu.make_async_remote_copy(
            src_ref=src,
            dst_ref=dst,
            send_sem=ssem.at[group],
            recv_sem=sem,
            device_id=to,
            device_id_type=MESH,
        ).start()

    def sent(ref, group):
        pltpu.make_async_remote_copy(
            src_ref=ref,
            dst_ref=ref,
            send_sem=ssem.at[group],
            recv_sem=rhalf.at[0],
            device_id=up,
            device_id_type=MESH,
        ).wait_send()

    def arrived(dst, sem):
        pltpu.make_async_remote_copy(
            src_ref=dst,
            dst_ref=dst,
            send_sem=ssem.at[0],
            recv_sem=sem,
            device_id=up,
            device_id_type=MESH,
        ).wait_recv()

    def local(src, dst, n):
        copy = pltpu.make_async_copy(src, dst, lsem.at[n])
        copy.start()
        return copy

    near = [up, down, across, beside, sibling, corner, along(1), along(7)]
    barrier = pltpu.get_barrier_semaphore()
    for peer in near:
        pl.semaphore_signal(barrier, inc=1, device_id=peer, device_id_type=MESH)
    loads = [
        local(cols_in, cols, 0),
        local(count_in, count, 1),
        local(w1_in, w1, 7),
        local(w2_in, w2, 4),
        local(feats_in, feats, 2),
        local(cot_in, cot, 5),
        local(vals_in.at[pl.ds(0, 8)], vals[0].at[pl.ds(c * 8, 8)], 6),
        local(vals_in.at[pl.ds(8, 8)], vals[1].at[pl.ds(c * 8, 8)], 3),
    ]
    pl.semaphore_wait(barrier, len(near))

    for k in (1, 7):
        pl.semaphore_signal(news.at[0], inc=1, device_id=along(k), device_id_type=MESH)

    def hear_far():
        pl.semaphore_wait(news.at[0], 2)
        for k in (2, 6):
            pl.semaphore_signal(news.at[1], inc=1, device_id=along(k), device_id_type=MESH)

    def spread(src, full, which):
        for peer in col_peers:
            send(src, full.at[c], rcol.at[which], peer, 3 + which)

    def collect(full, which):
        arrived(full.at[pl.ds(0, 7)], rcol.at[which])

    def part(q, r):
        return vals[r // 2].at[pl.ds(q * 8 + r % 2 * MINE, MINE)]

    def second_half(q):
        return vals[1].at[pl.ds(q * 8 + MINE + 2, 2)]

    def send_own(r, to):
        send(vals_in.at[pl.ds(r * MINE, MINE)], part(c, r), rvals.at[c, r], to, 0)

    for r in range(ROWS):
        send_own(r, up)
        send_own((2, 3, 0, 1)[r], down)
        send_own(r, across)

    below, above = col_at(xhi, y + 3), col_at(xhi, y + 1)
    partner, opposite = col_at(1 - xhi, y), col_at(xhi, y + 2)
    far_below, far_above = col_at(1 - xhi, y + 3), col_at(1 - xhi, y + 1)
    far_opposite = col_at(1 - xhi, y + 2)

    def take(q, r):
        arrived(part(q, r), rvals.at[q, r])

    def pass_on(q, r, to):
        send(part(q, r), part(q, r), rvals.at[q, r], to, 1)

    def forward(q, r, to):
        take(q, r)
        if to is not None:
            pass_on(q, r, to)

    def both_ways(r):
        take(partner, r)
        piece = part(partner, r)
        send(piece, piece, rvals.at[partner, r], up, 1)
        send(piece, piece, rvals.at[partner, r], down, 1)

    def at_block(v, xl, zz, cc):
        return v.at[pl.ds(cc * 64 + (xl * 8 + zz) * 4, 4)]

    def gather_start(v, which, far):
        mine = at_block(v, xlo, z, core)
        send(mine, mine, rgather.at[which, 0], beside, 2 + 4 * which)
        for i in range(7):
            sem = rgather.at[which, 2 if i >= far else 4 + i]
            send(mine, mine, sem, along(far_first(i)), 2 + 4 * which)

    def gather_second(v, which, far):
        other = at_block(v, 1 - xlo, z, core)
        arrived(other, rgather.at[which, 0])
        for i in range(far, 7):
            send(other, other, rgather.at[which, 3], along(far_first(i)), 2 + 4 * which)

    def gather_relay(v, which, far):
        for i in range(far):
            piece = at_block(v, xlo, (z + 8 - far_first(i)) % 8, core)
            arrived(piece, rgather.at[which, 4 + i])
            send(piece, piece, rgather.at[which, 3], beside, 2 + 4 * which)

    def gather_share(v, which, far):
        arrived(v.at[pl.ds(0, 4 * (7 - far))], rgather.at[which, 2])
        arrived(v.at[pl.ds(0, 28)], rgather.at[which, 3])
        half = v.at[pl.ds(core * 64, 64)]
        send(half, half, rgather.at[which, 1], sibling, 2 + 4 * which)

    def gather_finish(v, which):
        arrived(v.at[pl.ds(0, 64)], rgather.at[which, 1])

    def put_blocks(v, value):
        base = core * 64 + (xlo * 8 + z) * 4
        for b in range(4):
            v[base + b] = value[:, b * BLK : (b + 1) * BLK].astype(BF)

    def joined(ref):
        return ref[...].reshape(F, ROWS * BLK)

    def block_of(r, k):
        p = cols[r, k]
        return jnp.where(k < count[r], p // 4 % 2 * 64 + p // 8 * 4 + p % 4, NBLK)

    def product(v, rows):
        def step(q, totals):
            totals = list(totals)
            for n, r in enumerate(rows):
                for s in range(0, MINE, 2):
                    b = q * 8 + r % 2 * MINE + s
                    k = q * MINE + s
                    left = jnp.concatenate([v[block_of(r, k)], v[block_of(r, k + 1)]], axis=1)
                    right = jnp.concatenate([vals[r // 2][b], vals[r // 2][b + 1]], axis=1)
                    totals[n] = totals[n] + nt(left, right)
            return tuple(totals)

        zero = jnp.zeros((WIDE, BLK), F32)
        unroll = 4 if len(rows) > 2 else 8
        return lax.fori_loop(0, 8, step, (zero,) * len(rows), unroll=unroll)

    def term(g, pair, half, xl, i):
        p = dom_at(xl, (z + far_first(i)) % 8, half) * 4
        held, r = vals[pair], 2 * pair
        sums = []
        for b in range(0, 4, 2):
            right = jnp.concatenate(
                [
                    jnp.concatenate(
                        [held[inv[r + e, p + b]], held[inv[r + e, p + b + 1]]], axis=1
                    )
                    for e in range(2)
                ],
                axis=0,
            )
            got = jnp.dot(
                g[:, r * BLK : (r + 2) * BLK], right, preferred_element_type=F32
            )
            sums += [got[:, :BLK], got[:, BLK:]]
        return jnp.stack(sums)

    def over(at, n, write):
        def one(i, unused):
            write(i)
            return unused

        lax.fori_loop(at, at + n, one, 0, unroll=4)

    to_core, from_core, to_beside, from_beside, to_z, from_z, kept, early = bufs

    def first_rows(g):
        for n in range(4):
            half = 1 - core if n < 2 else core
            xl = xlo if n % 2 else 1 - xlo

            def one(i):
                early[n * 8 + i] = term(g, 0, half, xl, i)

            over(0, 8, one)

    def transposed(g, meanwhile):
        meanwhile[0]()
        for group in range(4):
            xl = 1 - xlo if group < 2 else xlo

            def one(i):
                at = group // 2 * 8 + i
                to_core[at] = (early[at] + term(g, 1, 1 - core, xl, i)).astype(BF)

            over(group % 2 * 4, 4, one)
            span = pl.ds(group * 4, 4)
            send(to_core.at[span], from_core.at[span], rred.at[group], sibling, 7)
        for group in range(4):
            if group % 2 == 0:
                arrived(from_core.at[pl.ds(group * 2, 4)], rred.at[group // 2])

            def two(i):
                total = early[16 + i] + term(g, 1, core, 1 - xlo, i)
                to_beside[i] = (total + from_core[i].astype(F32)).astype(BF)

            over(group * 2, 2, two)
            span = pl.ds(group * 2, 2)
            send(to_beside.at[span], from_beside.at[span], rred.at[4 + group], beside, 8)
        for group in range(2):
            arrived(from_core.at[pl.ds(8 + group * 4, 4)], rred.at[2 + group])

            def three(i):
                total = early[24 + i] + term(g, 1, core, xlo, i)
                kept[i] = total + from_core[8 + i].astype(F32)

            over(group * 4, 4, three)
        for group in range(4):
            if group == MEANWHILE:
                meanwhile[1]()
            arrived(from_beside.at[pl.ds(group * 2, 2)], rred.at[4 + group])
            for i in range(group * 2, group * 2 + 2):
                total = kept[i] + from_beside[i].astype(F32)
                if i < 7:
                    to_z[i] = total.astype(BF)
                    send(to_z.at[i], from_z.at[i], rred.at[8], along(far_first(i)), 9)
        kept[7] = total
        if MEANWHILE > 3:
            meanwhile[1]()
        total = kept[7]
        arrived(from_z.at[pl.ds(0, 7)], rred.at[8])
        for i in range(7):
            total = total + from_z[i].astype(F32)
        return jnp.concatenate([total[b] for b in range(4)], axis=1).astype(BF)

    zero_block = jnp.zeros((1, BLK, BLK), BF)
    vals[0][pl.ds(64, 1)] = zero_block
    vals[1][pl.ds(64, 1)] = zero_block
    v1[pl.ds(NBLK, 1)] = zero_block[:, :WIDE]
    v2[pl.ds(NBLK, 1)] = zero_block[:, :WIDE]
    hear_far()
    for copy in loads:
        copy.wait()
    put_blocks(v1, feats[...])
    pl.semaphore_wait(news.at[1], 2)
    gather_start(v1, 0, 0)
    lane = lax.broadcasted_iota(jnp.int32, (1, NBLK), 1)
    for r in range(ROWS):

        def mark(k, found):
            place = k // MINE * 8 + r % 2 * MINE + k % MINE - 64
            return found + jnp.where((lane == cols[r, k]) & (k < count[r]), place, 0)

        empty = jnp.full((1, NBLK), 64, jnp.int32)
        inv_rows[r : r + 1] = lax.fori_loop(0, 32, mark, empty, unroll=8)
    to_scalars = local(inv_rows, inv, 0)
    forward(below, 0, up)
    forward(above, 2, down)
    gather_second(v1, 0, 0)
    both_ways(0)
    forward(below, 1, up)
    forward(above, 3, down)
    forward(opposite, 0, across)
    forward(opposite, 2, across)
    w1_t[...] = w1[...].T
    w2_t[...] = w2[...].T
    both_ways(1)
    forward(opposite, 1, across)
    forward(opposite, 3, across)
    both_ways(2)
    both_ways(3)
    take(below, 3)
    take(above, 1)
    take(above, 0)
    take(below, 2)
    gather_share(v1, 0, 0)
    gather_finish(v1, 0)
    to_scalars.wait()

    def far_row(r):
        take(far_opposite, r)
        for n, q in enumerate((far_below, far_above)):
            take(q, r)

    def aggregate(rows):
        for r, total in zip(rows, product(v1, rows)):
            agg[c, :, r * BLK : (r + 1) * BLK] = total.astype(BF)

    far_row(0)
    far_row(1)
    aggregate((0, 1))
    cotangent = cot[...]
    first_rows(cotangent)
    far_row(2)
    aggregate((2,))
    far_row(3)
    mine = pl.ds(c * WIDE, WIDE)

    def last_row():
        aggregate((3,))
        spread(agg.at[c], agg, 0)

    def after_agg():
        collect(agg, 0)
        value = jnp.dot(w1_t[mine, :], joined(agg), preferred_element_type=F32)
        first[...] = value
        hid[c] = (value * jax.nn.sigmoid(value)).astype(BF)
        spread(hid.at[c], hid, 1)

    back[c] = transposed(cotangent, (last_row, after_agg))
    spread(back.at[c], back, 2)

    collect(hid, 1)
    put_blocks(v2, jnp.dot(w2_t[mine, :], joined(hid), preferred_element_type=F32))
    gather_start(v2, 1, 3)

    me = xlo * 2 + core
    pair = [
        (beside, (1 - xlo) * 2 + core),
        (sibling, xlo * 2 + 1 - core),
        (corner, (1 - xlo) * 2 + 1 - core),
    ]

    terms, quarters, along_z, whole = gbufs

    def quarters_out(n, grad):
        for k in range(4):
            terms[n, k] = grad[k * 8 : k * 8 + 8]
        for i, (to, k) in enumerate(pair):
            send(terms.at[n, k], quarters.at[n, i], rgrad.at[n], to, 10 + n)

    def sums_out():
        sums = []
        for n in range(2):
            total = terms[n, me]
            arrived(quarters.at[n], rgrad.at[n])
            for i in range(3):
                total = total + quarters[n, i]
            sums.append(total)
        along_z[7] = jnp.concatenate(sums, axis=0).astype(BF)
        for i in range(7):
            send(along_z.at[7], along_z.at[i], rgrad.at[2], along(far_first(i)), 12)

    def totals_out():
        arrived(along_z.at[pl.ds(0, 7)], rgrad.at[2])
        total = along_z[7].astype(F32)
        for i in range(7):
            total = total + along_z[i].astype(F32)
        whole[me] = total
        for to, k in pair:
            send(whole.at[me], whole.at[me], rgrad.at[3], to, 13)

    def totals_in():
        arrived(whole.at[pl.ds(0, 3)], rgrad.at[3])
        for k in range(4):
            for n in range(2):
                grads_ref[n, k * 8 : k * 8 + 8] = whole[k, n * 8 : n * 8 + 8]

    quarters_out(0, nt(back[c], joined(hid)))
    gather_second(v2, 1, 3)

    collect(back, 2)
    hidden_grad = jnp.dot(w2[mine, :], joined(back), preferred_element_type=F32)
    value = first[...]
    sig = jax.nn.sigmoid(value)
    act_grad = (hidden_grad * (sig + value * sig * (1.0 - sig))).astype(BF)
    quarters_out(1, nt(act_grad, joined(agg)))
    gather_relay(v2, 1, 3)
    sums_out()

    gather_share(v2, 1, 3)
    totals_out()
    gather_finish(v2, 1)
    for r, total in enumerate(product(v2, range(ROWS))):
        out_ref[:, r * BLK : (r + 1) * BLK] = total
    totals_in()
    sent(vals[0].at[pl.ds(0, 48)], 0)
    sent(vals[0].at[pl.ds(0, 64)], 1)
    sent(v1.at[pl.ds(0, 124)], 2)
    for n, full in enumerate((agg, hid, back)):
        sent(full.at[pl.ds(0, 7)], 3 + n)
    sent(v2.at[pl.ds(0, 124)], 6)
    sent(to_core, 7)
    sent(to_beside, 8)
    sent(to_z.at[pl.ds(0, 7)], 9)
    for n in range(2):
        sent(terms.at[n, pl.ds(0, 3)], 10 + n)
    sent(along_z.at[pl.ds(0, 7)], 12)
    sent(whole.at[pl.ds(0, 3)], 13)


def body(feats, w_first, w_second, block_cols, block_count, block_vals, cotangent):
    def blocks(n, kind):
        return pltpu.VMEM((n, 4, WIDE, BLK), kind)

    reduce_bufs = [blocks(n, BF) for n in (16, 16, 8, 8, 8, 8)]
    grad_bufs = [
        pltpu.VMEM((2, 4, 8, F), F32),
        pltpu.VMEM((2, 3, 8, F), F32),
        pltpu.VMEM((8, 16, F), BF),
        pltpu.VMEM((4, 16, F), F32),
    ]
    vmem = pl.BlockSpec(memory_space=pltpu.VMEM)
    anywhere = pl.BlockSpec(memory_space=pl.ANY)
    wide = pltpu.VMEM((8, WIDE, ROWS * BLK), BF)
    square = pltpu.VMEM((F, F), BF)
    dma = pltpu.SemaphoreType.DMA
    out, grads = pl.pallas_call(
        kernel,
        out_shape=(
            jax.ShapeDtypeStruct((WIDE, ROWS * BLK), F32),
            jax.ShapeDtypeStruct((2, WIDE, F), F32),
        ),
        in_specs=[anywhere] * 7,
        out_specs=(vmem, vmem),
        scratch_shapes=[
            [pltpu.VMEM((NBLK // 2 + 1, BLK, BLK), BF)] * 2,
            pltpu.VMEM((WIDE, ROWS * BLK), BF),
            wide,
            wide,
            wide,
            pltpu.VMEM((WIDE, ROWS * BLK), F32),
            pltpu.VMEM((NBLK + 1, WIDE, BLK), BF),
            pltpu.VMEM((NBLK + 1, WIDE, BLK), BF),
            square,
            square,
            square,
            square,
            pltpu.VMEM((WIDE, ROWS * BLK), BF),
            pltpu.VMEM((ROWS, NBLK), jnp.int32),
            pltpu.SMEM((ROWS, 32), jnp.int32),
            pltpu.SMEM((ROWS,), jnp.int32),
            pltpu.SMEM((ROWS, NBLK), jnp.int32),
            reduce_bufs + [blocks(8, F32), blocks(32, F32)],
            grad_bufs,
            dma((14,)),
            dma((8, 4)),
            dma((3,)),
            dma((2, 7)),
            dma((9,)),
            dma((4,)),
            dma((8,)),
            dma((2,)),
            pltpu.SemaphoreType.REGULAR((2,)),
        ],
        compiler_params=pltpu.CompilerParams(
            collective_id=0, has_side_effects=True, vmem_limit_bytes=56 << 20
        ),
        name="graph_layers",
    )(
        feats.T,
        cotangent.T,
        w_first,
        w_second,
        block_vals.reshape(ROWS * MINE, BLK, BLK),
        block_cols,
        block_count,
    )
    return (out.T, grads[1].T, grads[0].T)


def solution(mesh):
    return jax.shard_map(
        body,
        mesh=mesh,
        in_specs=(
            P("dom", "col"),
            P(),
            P(),
            P("dom", None),
            P("dom"),
            P("dom", "col", None, None),
            P("dom", "col"),
        ),
        out_specs=(P("dom", "col"), P(None, "col"), P(None, "col")),
        check_vma=False,
    )
```

```python
import functools

import jax
import jax.numpy as jnp
from jax import lax
from jax.experimental import pallas as pl
from jax.experimental.pallas import tpu as pltpu
from jax.sharding import PartitionSpec as P

BLK = 128
ROWS = 4
MINE = 4
NBLK = 128
MEANWHILE = 4
WIDE = 32
F = 256
MESH = pl.DeviceIdType.MESH
BF = jnp.bfloat16
F32 = jnp.float32


def far_first(i):
    return 4 + ((i + 1) // 2) * (1 - 2 * (i % 2))


def nt(a, b):
    return lax.dot_general(a, b, (((1,), (1,)), ((), ())), preferred_element_type=F32)


def kernel(
    feats_in,
    cot_in,
    w1_in,
    w2_in,
    vals_in,
    cols_in,
    count_in,
    out_ref,
    grads_ref,
    vals,
    feats,
    agg,
    hid,
    back,
    first,
    v1,
    v2,
    w1,
    w2,
    w1_t,
    w2_t,
    cot,
    inv_rows,
    cols,
    count,
    inv,
    bufs,
    gbufs,
    ssem,
    rvals,
    rcol,
    rgather,
    rred,
    rgrad,
    lsem,
    rhalf,
    news,
):
    d, c = lax.axis_index("dom"), lax.axis_index("col")
    xlo, z, core = d // 16, (d // 2) % 8, d % 2
    xhi, y = c // 4, c % 4

    def dom_at(xl, zz, cc):
        return (xl * 8 + zz) * 2 + cc

    def col_at(xh, yy):
        return xh * 4 + yy % 4

    up, down = (d, col_at(xhi, y + 1)), (d, col_at(xhi, y + 3))
    across = (d, col_at(1 - xhi, y))
    beside = (dom_at(1 - xlo, z, core), c)
    sibling = (dom_at(xlo, z, 1 - core), c)
    corner = (dom_at(1 - xlo, z, 1 - core), c)

    def along(k):
        return (dom_at(xlo, (z + k) % 8, core), c)

    col_peers = [
        (d, col_at((xhi + a) % 2, y + b)) for a in range(2) for b in range(4) if a + b
    ]

    def send(src, dst, sem, to, group):
        pltpu.make_async_remote_copy(
            src_ref=src,
            dst_ref=dst,
            send_sem=ssem.at[group],
            recv_sem=sem,
            device_id=to,
            device_id_type=MESH,
        ).start()

    def sent(ref, group):
        pltpu.make_async_remote_copy(
            src_ref=ref,
            dst_ref=ref,
            send_sem=ssem.at[group],
            recv_sem=rhalf.at[0],
            device_id=up,
            device_id_type=MESH,
        ).wait_send()

    def arrived(dst, sem):
        pltpu.make_async_remote_copy(
            src_ref=dst,
            dst_ref=dst,
            send_sem=ssem.at[0],
            recv_sem=sem,
            device_id=up,
            device_id_type=MESH,
        ).wait_recv()

    def local(src, dst, n):
        copy = pltpu.make_async_copy(src, dst, lsem.at[n])
        copy.start()
        return copy

    near = [up, down, across, beside, sibling, corner, along(1), along(7)]
    barrier = pltpu.get_barrier_semaphore()
    for peer in near:
        pl.semaphore_signal(barrier, inc=1, device_id=peer, device_id_type=MESH)
    loads = [
        local(cols_in, cols, 0),
        local(count_in, count, 1),
        local(w1_in, w1, 7),
        local(w2_in, w2, 4),
        local(feats_in, feats, 2),
        local(cot_in, cot, 5),
        local(vals_in.at[pl.ds(0, 8)], vals[0].at[pl.ds(c * 8, 8)], 6),
        local(vals_in.at[pl.ds(8, 8)], vals[1].at[pl.ds(c * 8, 8)], 3),
    ]
    pl.semaphore_wait(barrier, len(near))

    for k in (1, 7):
        pl.semaphore_signal(news.at[0], inc=1, device_id=along(k), device_id_type=MESH)

    def hear_far():
        pl.semaphore_wait(news.at[0], 2)
        for k in (2, 6):
            pl.semaphore_signal(news.at[1], inc=1, device_id=along(k), device_id_type=MESH)

    def spread(src, full, which):
        for peer in col_peers:
            send(src, full.at[c], rcol.at[which], peer, 3 + which)

    def collect(full, which):
        arrived(full.at[pl.ds(0, 7)], rcol.at[which])

    def part(q, r):
        return vals[r // 2].at[pl.ds(q * 8 + r % 2 * MINE, MINE)]

    def second_half(q):
        return vals[1].at[pl.ds(q * 8 + MINE + 2, 2)]

    def send_own(r, to):
        send(vals_in.at[pl.ds(r * MINE, MINE)], part(c, r), rvals.at[c, r], to, 0)

    for r in range(2):
        send_own(r, up)
        send_own(2 + r, down)
        send_own(r, across)
    for r in range(2, 4):
        send_own(r, across)

    below, above = col_at(xhi, y + 3), col_at(xhi, y + 1)
    partner, opposite = col_at(1 - xhi, y), col_at(xhi, y + 2)
    far_below, far_above = col_at(1 - xhi, y + 3), col_at(1 - xhi, y + 1)
    far_opposite = col_at(1 - xhi, y + 2)

    def take(q, r):
        arrived(part(q, r), rvals.at[q, r])

    def pass_on(q, r, to):
        send(part(q, r), part(q, r), rvals.at[q, r], to, 1)

    def forward(q, r, to):
        take(q, r)
        if to is not None:
            pass_on(q, r, to)

    def both_ways(r):
        take(partner, r)
        piece = part(partner, r)
        if r == 3:
            piece = piece.at[pl.ds(0, 2)]
        send(piece, piece, rvals.at[partner, r], up, 1)
        send(piece, piece, rvals.at[partner, r], down, 1)

    def at_block(v, xl, zz, cc):
        return v.at[pl.ds(cc * 64 + (xl * 8 + zz) * 4, 4)]

    def gather_start(v, which, far):
        mine = at_block(v, xlo, z, core)
        send(mine, mine, rgather.at[which, 0], beside, 2 + 4 * which)
        for i in range(7):
            sem = rgather.at[which, 2 if i >= far else 4 + i]
            send(mine, mine, sem, along(far_first(i)), 2 + 4 * which)

    def gather_second(v, which, far):
        other = at_block(v, 1 - xlo, z, core)
        arrived(other, rgather.at[which, 0])
        for i in range(far, 7):
            send(other, other, rgather.at[which, 3], along(far_first(i)), 2 + 4 * which)

    def gather_relay(v, which, far):
        for i in range(far):
            piece = at_block(v, xlo, (z + 8 - far_first(i)) % 8, core)
            arrived(piece, rgather.at[which, 4 + i])
            send(piece, piece, rgather.at[which, 3], beside, 2 + 4 * which)

    def gather_share(v, which, far):
        arrived(v.at[pl.ds(0, 4 * (7 - far))], rgather.at[which, 2])
        arrived(v.at[pl.ds(0, 28)], rgather.at[which, 3])
        half = v.at[pl.ds(core * 64, 64)]
        send(half, half, rgather.at[which, 1], sibling, 2 + 4 * which)

    def gather_finish(v, which):
        arrived(v.at[pl.ds(0, 64)], rgather.at[which, 1])

    def put_blocks(v, value):
        base = core * 64 + (xlo * 8 + z) * 4
        for b in range(4):
            v[base + b] = value[:, b * BLK : (b + 1) * BLK].astype(BF)

    def joined(ref):
        return ref[...].reshape(F, ROWS * BLK)

    def block_of(r, k):
        p = cols[r, k]
        return jnp.where(k < count[r], p // 4 % 2 * 64 + p // 8 * 4 + p % 4, NBLK)

    def product(v, rows):
        def step(q, totals):
            totals = list(totals)
            for n, r in enumerate(rows):
                for s in range(0, MINE, 2):
                    b = q * 8 + r % 2 * MINE + s
                    k = q * MINE + s
                    left = jnp.concatenate([v[block_of(r, k)], v[block_of(r, k + 1)]], axis=1)
                    right = jnp.concatenate([vals[r // 2][b], vals[r // 2][b + 1]], axis=1)
                    totals[n] = totals[n] + nt(left, right)
            return tuple(totals)

        zero = jnp.zeros((WIDE, BLK), F32)
        unroll = 4 if len(rows) > 2 else 8
        return lax.fori_loop(0, 8, step, (zero,) * len(rows), unroll=unroll)

    def term(g, pair, half, xl, i):
        p = dom_at(xl, (z + far_first(i)) % 8, half) * 4
        held, r = vals[pair], 2 * pair
        sums = []
        for b in range(0, 4, 2):
            right = jnp.concatenate(
                [
                    jnp.concatenate(
                        [held[inv[r + e, p + b]], held[inv[r + e, p + b + 1]]], axis=1
                    )
                    for e in range(2)
                ],
                axis=0,
            )
            got = jnp.dot(
                g[:, r * BLK : (r + 2) * BLK], right, preferred_element_type=F32
            )
            sums += [got[:, :BLK], got[:, BLK:]]
        return jnp.stack(sums)

    def over(at, n, write):
        def one(i, unused):
            write(i)
            return unused

        lax.fori_loop(at, at + n, one, 0, unroll=4)

    to_core, from_core, to_beside, from_beside, to_z, from_z, kept, early = bufs

    def first_rows(g):
        for n in range(4):
            half = 1 - core if n < 2 else core
            xl = xlo if n % 2 else 1 - xlo

            def one(i):
                early[n * 8 + i] = term(g, 0, half, xl, i)

            over(0, 8, one)

    def transposed(g, meanwhile):
        meanwhile[0]()
        for group in range(4):
            xl = 1 - xlo if group < 2 else xlo

            def one(i):
                at = group // 2 * 8 + i
                to_core[at] = (early[at] + term(g, 1, 1 - core, xl, i)).astype(BF)

            over(group % 2 * 4, 4, one)
            span = pl.ds(group * 4, 4)
            send(to_core.at[span], from_core.at[span], rred.at[group], sibling, 7)
        for group in range(4):
            if group % 2 == 0:
                arrived(from_core.at[pl.ds(group * 2, 4)], rred.at[group // 2])

            def two(i):
                total = early[16 + i] + term(g, 1, core, 1 - xlo, i)
                to_beside[i] = (total + from_core[i].astype(F32)).astype(BF)

            over(group * 2, 2, two)
            span = pl.ds(group * 2, 2)
            send(to_beside.at[span], from_beside.at[span], rred.at[4 + group], beside, 8)
        for group in range(2):
            arrived(from_core.at[pl.ds(8 + group * 4, 4)], rred.at[2 + group])

            def three(i):
                total = early[24 + i] + term(g, 1, core, xlo, i)
                kept[i] = total + from_core[8 + i].astype(F32)

            over(group * 4, 4, three)
        for group in range(4):
            if group == MEANWHILE:
                meanwhile[1]()
            arrived(from_beside.at[pl.ds(group * 2, 2)], rred.at[4 + group])
            for i in range(group * 2, group * 2 + 2):
                total = kept[i] + from_beside[i].astype(F32)
                if i < 7:
                    to_z[i] = total.astype(BF)
                    send(to_z.at[i], from_z.at[i], rred.at[8], along(far_first(i)), 9)
        kept[7] = total
        if MEANWHILE > 3:
            meanwhile[1]()
        total = kept[7]
        arrived(from_z.at[pl.ds(0, 7)], rred.at[8])
        for i in range(7):
            total = total + from_z[i].astype(F32)
        return jnp.concatenate([total[b] for b in range(4)], axis=1).astype(BF)

    zero_block = jnp.zeros((1, BLK, BLK), BF)
    vals[0][pl.ds(64, 1)] = zero_block
    vals[1][pl.ds(64, 1)] = zero_block
    v1[pl.ds(NBLK, 1)] = zero_block[:, :WIDE]
    v2[pl.ds(NBLK, 1)] = zero_block[:, :WIDE]
    hear_far()
    for copy in loads:
        copy.wait()
    put_blocks(v1, feats[...])
    pl.semaphore_wait(news.at[1], 2)
    gather_start(v1, 0, 0)
    lane = lax.broadcasted_iota(jnp.int32, (1, NBLK), 1)
    for r in range(ROWS):

        def mark(k, found):
            place = k // MINE * 8 + r % 2 * MINE + k % MINE - 64
            return found + jnp.where((lane == cols[r, k]) & (k < count[r]), place, 0)

        empty = jnp.full((1, NBLK), 64, jnp.int32)
        inv_rows[r : r + 1] = lax.fori_loop(0, 32, mark, empty, unroll=8)
    to_scalars = local(inv_rows, inv, 0)
    forward(below, 0, up)
    forward(above, 2, down)
    forward(below, 1, up)
    forward(above, 3, down)
    for r in range(2):
        send_own(2 + r, up)
        send_own(r, down)
    gather_second(v1, 0, 0)
    both_ways(0)
    forward(opposite, 0, across)
    forward(opposite, 2, across)
    both_ways(1)
    w1_t[...] = w1[...].T
    w2_t[...] = w2[...].T
    forward(opposite, 1, across)
    forward(opposite, 3, across)
    both_ways(2)
    both_ways(3)
    take(below, 3)
    send(second_half(below), second_half(below), rhalf.at[0], across, 14)
    send(second_half(above), second_half(above), rhalf.at[1], across, 14)
    take(above, 1)
    take(above, 0)
    take(below, 2)
    gather_share(v1, 0, 0)
    gather_finish(v1, 0)
    to_scalars.wait()

    def far_row(r):
        take(far_opposite, r)
        for n, q in enumerate((far_below, far_above)):
            if r == 3:
                arrived(vals[1].at[pl.ds(q * 8 + MINE, 2)], rvals.at[q, r])
                arrived(second_half(q), rhalf.at[n])
            else:
                take(q, r)

    def aggregate(rows):
        for r, total in zip(rows, product(v1, rows)):
            agg[c, :, r * BLK : (r + 1) * BLK] = total.astype(BF)

    far_row(0)
    far_row(1)
    aggregate((0, 1))
    cotangent = cot[...]
    first_rows(cotangent)
    far_row(2)
    aggregate((2,))
    far_row(3)
    mine = pl.ds(c * WIDE, WIDE)

    def last_row():
        aggregate((3,))
        spread(agg.at[c], agg, 0)

    def after_agg():
        collect(agg, 0)
        value = jnp.dot(w1_t[mine, :], joined(agg), preferred_element_type=F32)
        first[...] = value
        hid[c] = (value * jax.nn.sigmoid(value)).astype(BF)
        spread(hid.at[c], hid, 1)

    back[c] = transposed(cotangent, (last_row, after_agg))
    spread(back.at[c], back, 2)

    collect(hid, 1)
    put_blocks(v2, jnp.dot(w2_t[mine, :], joined(hid), preferred_element_type=F32))
    gather_start(v2, 1, 3)

    me = xlo * 2 + core
    pair = [
        (beside, (1 - xlo) * 2 + core),
        (sibling, xlo * 2 + 1 - core),
        (corner, (1 - xlo) * 2 + 1 - core),
    ]

    terms, quarters, along_z, whole = gbufs

    def quarters_out(n, grad):
        for k in range(4):
            terms[n, k] = grad[k * 8 : k * 8 + 8]
        for i, (to, k) in enumerate(pair):
            send(terms.at[n, k], quarters.at[n, i], rgrad.at[n], to, 10 + n)

    def sums_out():
        sums = []
        for n in range(2):
            total = terms[n, me]
            arrived(quarters.at[n], rgrad.at[n])
            for i in range(3):
                total = total + quarters[n, i]
            sums.append(total)
        along_z[7] = jnp.concatenate(sums, axis=0).astype(BF)
        for i in range(7):
            send(along_z.at[7], along_z.at[i], rgrad.at[2], along(far_first(i)), 12)

    def totals_out():
        arrived(along_z.at[pl.ds(0, 7)], rgrad.at[2])
        total = along_z[7].astype(F32)
        for i in range(7):
            total = total + along_z[i].astype(F32)
        whole[me] = total
        for to, k in pair:
            send(whole.at[me], whole.at[me], rgrad.at[3], to, 13)

    def totals_in():
        arrived(whole.at[pl.ds(0, 3)], rgrad.at[3])
        for k in range(4):
            for n in range(2):
                grads_ref[n, k * 8 : k * 8 + 8] = whole[k, n * 8 : n * 8 + 8]

    quarters_out(0, nt(back[c], joined(hid)))
    gather_second(v2, 1, 3)

    collect(back, 2)
    hidden_grad = jnp.dot(w2[mine, :], joined(back), preferred_element_type=F32)
    value = first[...]
    sig = jax.nn.sigmoid(value)
    act_grad = (hidden_grad * (sig + value * sig * (1.0 - sig))).astype(BF)
    quarters_out(1, nt(act_grad, joined(agg)))
    gather_relay(v2, 1, 3)
    sums_out()

    gather_share(v2, 1, 3)
    totals_out()
    gather_finish(v2, 1)
    for r, total in enumerate(product(v2, range(ROWS))):
        out_ref[:, r * BLK : (r + 1) * BLK] = total
    totals_in()
    sent(vals[0].at[pl.ds(0, 48)], 0)
    sent(vals[0].at[pl.ds(0, 60)], 1)
    sent(vals[0].at[pl.ds(0, 4)], 14)
    sent(v1.at[pl.ds(0, 124)], 2)
    for n, full in enumerate((agg, hid, back)):
        sent(full.at[pl.ds(0, 7)], 3 + n)
    sent(v2.at[pl.ds(0, 124)], 6)
    sent(to_core, 7)
    sent(to_beside, 8)
    sent(to_z.at[pl.ds(0, 7)], 9)
    for n in range(2):
        sent(terms.at[n, pl.ds(0, 3)], 10 + n)
    sent(along_z.at[pl.ds(0, 7)], 12)
    sent(whole.at[pl.ds(0, 3)], 13)


def body(feats, w_first, w_second, block_cols, block_count, block_vals, cotangent):
    def blocks(n, kind):
        return pltpu.VMEM((n, 4, WIDE, BLK), kind)

    reduce_bufs = [blocks(n, BF) for n in (16, 16, 8, 8, 8, 8)]
    grad_bufs = [
        pltpu.VMEM((2, 4, 8, F), F32),
        pltpu.VMEM((2, 3, 8, F), F32),
        pltpu.VMEM((8, 16, F), BF),
        pltpu.VMEM((4, 16, F), F32),
    ]
    vmem = pl.BlockSpec(memory_space=pltpu.VMEM)
    anywhere = pl.BlockSpec(memory_space=pl.ANY)
    wide = pltpu.VMEM((8, WIDE, ROWS * BLK), BF)
    square = pltpu.VMEM((F, F), BF)
    dma = pltpu.SemaphoreType.DMA
    out, grads = pl.pallas_call(
        kernel,
        out_shape=(
            jax.ShapeDtypeStruct((WIDE, ROWS * BLK), F32),
            jax.ShapeDtypeStruct((2, WIDE, F), F32),
        ),
        in_specs=[anywhere] * 7,
        out_specs=(vmem, vmem),
        scratch_shapes=[
            [pltpu.VMEM((NBLK // 2 + 1, BLK, BLK), BF)] * 2,
            pltpu.VMEM((WIDE, ROWS * BLK), BF),
            wide,
            wide,
            wide,
            pltpu.VMEM((WIDE, ROWS * BLK), F32),
            pltpu.VMEM((NBLK + 1, WIDE, BLK), BF),
            pltpu.VMEM((NBLK + 1, WIDE, BLK), BF),
            square,
            square,
            square,
            square,
            pltpu.VMEM((WIDE, ROWS * BLK), BF),
            pltpu.VMEM((ROWS, NBLK), jnp.int32),
            pltpu.SMEM((ROWS, 32), jnp.int32),
            pltpu.SMEM((ROWS,), jnp.int32),
            pltpu.SMEM((ROWS, NBLK), jnp.int32),
            reduce_bufs + [blocks(8, F32), blocks(32, F32)],
            grad_bufs,
            dma((15,)),
            dma((8, 4)),
            dma((3,)),
            dma((2, 7)),
            dma((9,)),
            dma((4,)),
            dma((8,)),
            dma((2,)),
            pltpu.SemaphoreType.REGULAR((2,)),
        ],
        compiler_params=pltpu.CompilerParams(
            collective_id=0, has_side_effects=True, vmem_limit_bytes=56 << 20
        ),
        name="graph_layers",
    )(
        feats.T,
        cotangent.T,
        w_first,
        w_second,
        block_vals.reshape(ROWS * MINE, BLK, BLK),
        block_cols,
        block_count,
    )
    return (out.T, grads[1].T, grads[0].T)


def solution(mesh):
    return jax.shard_map(
        body,
        mesh=mesh,
        in_specs=(
            P("dom", "col"),
            P(),
            P(),
            P("dom", None),
            P("dom"),
            P("dom", "col", None, None),
            P("dom", "col"),
        ),
        out_specs=(P("dom", "col"), P(None, "col"), P(None, "col")),
        check_vma=False,
    )
```

```python
import functools

import jax
import jax.numpy as jnp
from jax import lax
from jax.experimental import pallas as pl
from jax.experimental.pallas import tpu as pltpu
from jax.sharding import PartitionSpec as P

BLK = 128
ROWS = 4
MINE = 4
NBLK = 128
MEANWHILE = 3
WIDE = 32
F = 256
MESH = pl.DeviceIdType.MESH
BF = jnp.bfloat16
F32 = jnp.float32


def far_first(i):
    return 4 + ((i + 1) // 2) * (1 - 2 * (i % 2))


def nt(a, b):
    return lax.dot_general(a, b, (((1,), (1,)), ((), ())), preferred_element_type=F32)


def kernel(
    feats_in,
    cot_in,
    w1_in,
    w2_in,
    vals_in,
    cols_in,
    count_in,
    out_ref,
    vals,
    feats,
    agg,
    hid,
    back,
    first,
    v1,
    v2,
    w1,
    w2,
    w1_t,
    w2_t,
    cot,
    inv_rows,
    cols,
    count,
    inv,
    bufs,
    gbufs,
    ssem,
    rvals,
    rcol,
    rgather,
    rred,
    rgrad,
    lsem,
    rhalf,
    news,
):
    d, c = lax.axis_index("dom"), lax.axis_index("col")
    xlo, z, core = d // 16, (d // 2) % 8, d % 2
    xhi, y = c // 4, c % 4

    def dom_at(xl, zz, cc):
        return (xl * 8 + zz) * 2 + cc

    def col_at(xh, yy):
        return xh * 4 + yy % 4

    up, down = (d, col_at(xhi, y + 1)), (d, col_at(xhi, y + 3))
    across = (d, col_at(1 - xhi, y))
    beside = (dom_at(1 - xlo, z, core), c)
    sibling = (dom_at(xlo, z, 1 - core), c)
    corner = (dom_at(1 - xlo, z, 1 - core), c)

    def along(k):
        return (dom_at(xlo, (z + k) % 8, core), c)

    col_peers = [
        (d, col_at((xhi + a) % 2, y + b)) for a in range(2) for b in range(4) if a + b
    ]

    def send(src, dst, sem, to, group):
        pltpu.make_async_remote_copy(
            src_ref=src,
            dst_ref=dst,
            send_sem=ssem.at[group],
            recv_sem=sem,
            device_id=to,
            device_id_type=MESH,
        ).start()

    def sent(ref, group):
        pltpu.make_async_remote_copy(
            src_ref=ref,
            dst_ref=ref,
            send_sem=ssem.at[group],
            recv_sem=rhalf.at[0],
            device_id=up,
            device_id_type=MESH,
        ).wait_send()

    def arrived(dst, sem):
        pltpu.make_async_remote_copy(
            src_ref=dst,
            dst_ref=dst,
            send_sem=ssem.at[0],
            recv_sem=sem,
            device_id=up,
            device_id_type=MESH,
        ).wait_recv()

    def local(src, dst, n):
        copy = pltpu.make_async_copy(src, dst, lsem.at[n])
        copy.start()
        return copy

    near = [up, down, across, beside, sibling, corner, along(1), along(7)]
    barrier = pltpu.get_barrier_semaphore()
    for peer in near:
        pl.semaphore_signal(barrier, inc=1, device_id=peer, device_id_type=MESH)
    loads = [
        local(cols_in, cols, 0),
        local(count_in, count, 1),
        local(w1_in, w1, 7),
        local(w2_in, w2, 4),
        local(feats_in, feats, 2),
        local(cot_in, cot, 5),
        local(vals_in.at[pl.ds(0, 8)], vals[0].at[pl.ds(c * 8, 8)], 6),
        local(vals_in.at[pl.ds(8, 8)], vals[1].at[pl.ds(c * 8, 8)], 3),
    ]
    pl.semaphore_wait(barrier, len(near))

    for k in (1, 7):
        pl.semaphore_signal(news.at[0], inc=1, device_id=along(k), device_id_type=MESH)

    def hear_far():
        pl.semaphore_wait(news.at[0], 2)
        for k in (2, 6):
            pl.semaphore_signal(news.at[1], inc=1, device_id=along(k), device_id_type=MESH)

    def spread(src, full, which):
        for peer in col_peers:
            send(src, full.at[c], rcol.at[which], peer, 3 + which)

    def collect(full, which):
        arrived(full.at[pl.ds(0, 7)], rcol.at[which])

    def part(q, r):
        return vals[r // 2].at[pl.ds(q * 8 + r % 2 * MINE, MINE)]

    def second_half(q):
        return vals[1].at[pl.ds(q * 8 + MINE + 2, 2)]

    def send_own(r, to):
        send(vals_in.at[pl.ds(r * MINE, MINE)], part(c, r), rvals.at[c, r], to, 0)

    for r in range(2):
        send_own(r, up)
        send_own(2 + r, down)
        send_own(r, across)
    for r in range(2, 4):
        send_own(r, across)

    below, above = col_at(xhi, y + 3), col_at(xhi, y + 1)
    partner, opposite = col_at(1 - xhi, y), col_at(xhi, y + 2)
    far_below, far_above = col_at(1 - xhi, y + 3), col_at(1 - xhi, y + 1)
    far_opposite = col_at(1 - xhi, y + 2)

    def take(q, r):
        arrived(part(q, r), rvals.at[q, r])

    def pass_on(q, r, to):
        send(part(q, r), part(q, r), rvals.at[q, r], to, 1)

    def forward(q, r, to):
        take(q, r)
        if to is not None:
            pass_on(q, r, to)

    def both_ways(r):
        take(partner, r)
        piece = part(partner, r)
        if r == 3:
            piece = piece.at[pl.ds(0, 2)]
        send(piece, piece, rvals.at[partner, r], up, 1)
        send(piece, piece, rvals.at[partner, r], down, 1)

    def at_block(v, xl, zz, cc):
        return v.at[pl.ds(cc * 64 + (xl * 8 + zz) * 4, 4)]

    def gather_start(v, which, far):
        mine = at_block(v, xlo, z, core)
        send(mine, mine, rgather.at[which, 0], beside, 2 + 4 * which)
        for i in range(7):
            sem = rgather.at[which, 2 if i >= far else 4 + i]
            send(mine, mine, sem, along(far_first(i)), 2 + 4 * which)

    def gather_second(v, which, far):
        other = at_block(v, 1 - xlo, z, core)
        arrived(other, rgather.at[which, 0])
        for i in range(far, 7):
            send(other, other, rgather.at[which, 3], along(far_first(i)), 2 + 4 * which)

    def gather_relay(v, which, far):
        for i in range(far):
            piece = at_block(v, xlo, (z + 8 - far_first(i)) % 8, core)
            arrived(piece, rgather.at[which, 4 + i])
            send(piece, piece, rgather.at[which, 3], beside, 2 + 4 * which)

    def gather_share(v, which, far):
        arrived(v.at[pl.ds(0, 4 * (7 - far))], rgather.at[which, 2])
        arrived(v.at[pl.ds(0, 28)], rgather.at[which, 3])
        half = v.at[pl.ds(core * 64, 64)]
        send(half, half, rgather.at[which, 1], sibling, 2 + 4 * which)

    def gather_finish(v, which):
        arrived(v.at[pl.ds(0, 64)], rgather.at[which, 1])

    def put_blocks(v, value):
        base = core * 64 + (xlo * 8 + z) * 4
        for b in range(4):
            v[base + b] = value[:, b * BLK : (b + 1) * BLK].astype(BF)

    def joined(ref):
        return ref[...].reshape(F, ROWS * BLK)

    def block_of(r, k):
        p = cols[r, k]
        return jnp.where(k < count[r], p // 4 % 2 * 64 + p // 8 * 4 + p % 4, NBLK)

    def product(v, rows):
        def step(q, totals):
            totals = list(totals)
            for n, r in enumerate(rows):
                for s in range(0, MINE, 2):
                    b = q * 8 + r % 2 * MINE + s
                    k = q * MINE + s
                    left = jnp.concatenate([v[block_of(r, k)], v[block_of(r, k + 1)]], axis=1)
                    right = jnp.concatenate([vals[r // 2][b], vals[r // 2][b + 1]], axis=1)
                    totals[n] = totals[n] + nt(left, right)
            return tuple(totals)

        zero = jnp.zeros((WIDE, BLK), F32)
        unroll = 4 if len(rows) > 2 else 8
        return lax.fori_loop(0, 8, step, (zero,) * len(rows), unroll=unroll)

    def term(g, pair, half, xl, i):
        p = dom_at(xl, (z + far_first(i)) % 8, half) * 4
        held, r = vals[pair], 2 * pair
        sums = []
        for b in range(0, 4, 2):
            right = jnp.concatenate(
                [
                    jnp.concatenate(
                        [held[inv[r + e, p + b]], held[inv[r + e, p + b + 1]]], axis=1
                    )
                    for e in range(2)
                ],
                axis=0,
            )
            got = jnp.dot(
                g[:, r * BLK : (r + 2) * BLK], right, preferred_element_type=F32
            )
            sums += [got[:, :BLK], got[:, BLK:]]
        return jnp.stack(sums)

    def over(at, n, write):
        def one(i, unused):
            write(i)
            return unused

        lax.fori_loop(at, at + n, one, 0, unroll=4)

    to_core, from_core, to_beside, from_beside, to_z, from_z, kept, early = bufs

    def first_rows(g):
        for n in range(4):
            half = 1 - core if n < 2 else core
            xl = xlo if n % 2 else 1 - xlo

            def one(i):
                early[n * 8 + i] = term(g, 0, half, xl, i)

            over(0, 8, one)

    def transposed(g, meanwhile):
        meanwhile[0]()
        for group in range(4):
            xl = 1 - xlo if group < 2 else xlo

            def one(i):
                at = group // 2 * 8 + i
                to_core[at] = (early[at] + term(g, 1, 1 - core, xl, i)).astype(BF)

            over(group % 2 * 4, 4, one)
            span = pl.ds(group * 4, 4)
            send(to_core.at[span], from_core.at[span], rred.at[group], sibling, 7)
        for group in range(4):
            if group % 2 == 0:
                arrived(from_core.at[pl.ds(group * 2, 4)], rred.at[group // 2])

            def two(i):
                total = early[16 + i] + term(g, 1, core, 1 - xlo, i)
                to_beside[i] = (total + from_core[i].astype(F32)).astype(BF)

            over(group * 2, 2, two)
            span = pl.ds(group * 2, 2)
            send(to_beside.at[span], from_beside.at[span], rred.at[4 + group], beside, 8)
        for group in range(2):
            arrived(from_core.at[pl.ds(8 + group * 4, 4)], rred.at[2 + group])

            def three(i):
                total = early[24 + i] + term(g, 1, core, xlo, i)
                kept[i] = total + from_core[8 + i].astype(F32)

            over(group * 4, 4, three)
        for group in range(4):
            if group == MEANWHILE:
                meanwhile[1]()
            arrived(from_beside.at[pl.ds(group * 2, 2)], rred.at[4 + group])
            for i in range(group * 2, group * 2 + 2):
                total = kept[i] + from_beside[i].astype(F32)
                if i < 7:
                    to_z[i] = total.astype(BF)
                    send(to_z.at[i], from_z.at[i], rred.at[8], along(far_first(i)), 9)
        kept[7] = total
        if MEANWHILE > 3:
            meanwhile[1]()
        total = kept[7]
        arrived(from_z.at[pl.ds(0, 7)], rred.at[8])
        for i in range(7):
            total = total + from_z[i].astype(F32)
        return jnp.concatenate([total[b] for b in range(4)], axis=1).astype(BF)

    zero_block = jnp.zeros((1, BLK, BLK), BF)
    vals[0][pl.ds(64, 1)] = zero_block
    vals[1][pl.ds(64, 1)] = zero_block
    v1[pl.ds(NBLK, 1)] = zero_block[:, :WIDE]
    v2[pl.ds(NBLK, 1)] = zero_block[:, :WIDE]
    hear_far()
    for copy in loads:
        copy.wait()
    put_blocks(v1, feats[...])
    pl.semaphore_wait(news.at[1], 2)
    gather_start(v1, 0, 0)
    lane = lax.broadcasted_iota(jnp.int32, (1, NBLK), 1)
    for r in range(ROWS):

        def mark(k, found):
            place = k // MINE * 8 + r % 2 * MINE + k % MINE - 64
            return found + jnp.where((lane == cols[r, k]) & (k < count[r]), place, 0)

        empty = jnp.full((1, NBLK), 64, jnp.int32)
        inv_rows[r : r + 1] = lax.fori_loop(0, 32, mark, empty, unroll=8)
    to_scalars = local(inv_rows, inv, 0)
    forward(below, 0, up)
    forward(above, 2, down)
    forward(below, 1, up)
    forward(above, 3, down)
    for r in range(2):
        send_own(2 + r, up)
        send_own(r, down)
    gather_second(v1, 0, 0)
    both_ways(0)
    forward(opposite, 0, across)
    forward(opposite, 2, across)
    both_ways(1)
    w1_t[...] = w1[...].T
    w2_t[...] = w2[...].T
    forward(opposite, 1, across)
    forward(opposite, 3, across)
    both_ways(2)
    both_ways(3)
    take(below, 3)
    send(second_half(below), second_half(below), rhalf.at[0], across, 14)
    send(second_half(above), second_half(above), rhalf.at[1], across, 14)
    take(above, 1)
    take(above, 0)
    take(below, 2)
    gather_share(v1, 0, 0)
    gather_finish(v1, 0)
    to_scalars.wait()

    def far_row(r):
        take(far_opposite, r)
        for n, q in enumerate((far_below, far_above)):
            if r == 3:
                arrived(vals[1].at[pl.ds(q * 8 + MINE, 2)], rvals.at[q, r])
                arrived(second_half(q), rhalf.at[n])
            else:
                take(q, r)

    def aggregate(rows):
        for r, total in zip(rows, product(v1, rows)):
            agg[c, :, r * BLK : (r + 1) * BLK] = total.astype(BF)

    far_row(0)
    far_row(1)
    aggregate((0, 1))
    cotangent = cot[...]
    first_rows(cotangent)
    far_row(2)
    aggregate((2,))
    far_row(3)
    mine = pl.ds(c * WIDE, WIDE)

    def last_row():
        aggregate((3,))
        spread(agg.at[c], agg, 0)

    def after_agg():
        collect(agg, 0)
        value = jnp.dot(w1_t[mine, :], joined(agg), preferred_element_type=F32)
        first[...] = value
        hid[c] = (value * jax.nn.sigmoid(value)).astype(BF)
        spread(hid.at[c], hid, 1)

    back[c] = transposed(cotangent, (last_row, after_agg))
    spread(back.at[c], back, 2)

    collect(hid, 1)
    put_blocks(v2, jnp.dot(w2_t[mine, :], joined(hid), preferred_element_type=F32))
    gather_start(v2, 1, 3)

    me = xlo * 2 + core
    pair = [
        (beside, (1 - xlo) * 2 + core),
        (sibling, xlo * 2 + 1 - core),
        (corner, (1 - xlo) * 2 + 1 - core),
    ]

    terms, quarters, along_z, whole = gbufs

    def quarters_out(n, grad):
        for k in range(4):
            terms[n, k] = grad[k * 8 : k * 8 + 8]
        for i, (to, k) in enumerate(pair):
            send(terms.at[n, k], quarters.at[n, i], rgrad.at[n], to, 10 + n)

    def sums_out():
        sums = []
        for n in range(2):
            total = terms[n, me]
            arrived(quarters.at[n], rgrad.at[n])
            for i in range(3):
                total = total + quarters[n, i]
            sums.append(total)
        along_z[7] = jnp.concatenate(sums, axis=0).astype(BF)
        for i in range(7):
            send(along_z.at[7], along_z.at[i], rgrad.at[2], along(far_first(i)), 12)

    def totals_out():
        arrived(along_z.at[pl.ds(0, 7)], rgrad.at[2])
        total = along_z[7].astype(F32)
        for i in range(7):
            total = total + along_z[i].astype(F32)
        whole[me] = total
        for to, k in pair:
            send(whole.at[me], whole.at[me], rgrad.at[3], to, 13)

    def totals_in():
        arrived(whole.at[pl.ds(0, 3)], rgrad.at[3])
        for k in range(4):
            for n in range(2):
                out_ref[k * 8 : k * 8 + 8, ROWS * BLK + n * F : ROWS * BLK + n * F + F] = whole[k, n * 8 : n * 8 + 8]

    quarters_out(0, nt(back[c], joined(hid)))
    gather_second(v2, 1, 3)

    collect(back, 2)
    hidden_grad = jnp.dot(w2[mine, :], joined(back), preferred_element_type=F32)
    value = first[...]
    sig = jax.nn.sigmoid(value)
    act_grad = (hidden_grad * (sig + value * sig * (1.0 - sig))).astype(BF)
    quarters_out(1, nt(act_grad, joined(agg)))
    gather_relay(v2, 1, 3)
    sums_out()

    gather_share(v2, 1, 3)
    totals_out()
    gather_finish(v2, 1)
    for r, total in enumerate(product(v2, range(ROWS))):
        out_ref[:, r * BLK : (r + 1) * BLK] = total
    totals_in()
    sent(vals[0].at[pl.ds(0, 48)], 0)
    sent(vals[0].at[pl.ds(0, 60)], 1)
    sent(vals[0].at[pl.ds(0, 4)], 14)
    sent(v1.at[pl.ds(0, 124)], 2)
    for n, full in enumerate((agg, hid, back)):
        sent(full.at[pl.ds(0, 7)], 3 + n)
    sent(v2.at[pl.ds(0, 124)], 6)
    sent(to_core, 7)
    sent(to_beside, 8)
    sent(to_z.at[pl.ds(0, 7)], 9)
    for n in range(2):
        sent(terms.at[n, pl.ds(0, 3)], 10 + n)
    sent(along_z.at[pl.ds(0, 7)], 12)
    sent(whole.at[pl.ds(0, 3)], 13)


def body(feats, w_first, w_second, block_cols, block_count, block_vals, cotangent):
    def blocks(n, kind):
        return pltpu.VMEM((n, 4, WIDE, BLK), kind)

    reduce_bufs = [blocks(n, BF) for n in (16, 16, 8, 8, 8, 8)]
    grad_bufs = [
        pltpu.VMEM((2, 4, 8, F), F32),
        pltpu.VMEM((2, 3, 8, F), F32),
        pltpu.VMEM((8, 16, F), BF),
        pltpu.VMEM((4, 16, F), F32),
    ]
    vmem = pl.BlockSpec(memory_space=pltpu.VMEM)
    anywhere = pl.BlockSpec(memory_space=pl.ANY)
    wide = pltpu.VMEM((8, WIDE, ROWS * BLK), BF)
    square = pltpu.VMEM((F, F), BF)
    dma = pltpu.SemaphoreType.DMA
    (out,) = pl.pallas_call(
        kernel,
        out_shape=(
            jax.ShapeDtypeStruct((WIDE, ROWS * BLK + 2 * F), F32),
        ),
        in_specs=[anywhere] * 7,
        out_specs=(vmem,),
        scratch_shapes=[
            [pltpu.VMEM((NBLK // 2 + 1, BLK, BLK), BF)] * 2,
            pltpu.VMEM((WIDE, ROWS * BLK), BF),
            wide,
            wide,
            wide,
            pltpu.VMEM((WIDE, ROWS * BLK), F32),
            pltpu.VMEM((NBLK + 1, WIDE, BLK), BF),
            pltpu.VMEM((NBLK + 1, WIDE, BLK), BF),
            square,
            square,
            square,
            square,
            pltpu.VMEM((WIDE, ROWS * BLK), BF),
            pltpu.VMEM((ROWS, NBLK), jnp.int32),
            pltpu.SMEM((ROWS, 32), jnp.int32),
            pltpu.SMEM((ROWS,), jnp.int32),
            pltpu.SMEM((ROWS, NBLK), jnp.int32),
            reduce_bufs + [blocks(8, F32), blocks(32, F32)],
            grad_bufs,
            dma((15,)),
            dma((8, 4)),
            dma((3,)),
            dma((2, 7)),
            dma((9,)),
            dma((4,)),
            dma((8,)),
            dma((2,)),
            pltpu.SemaphoreType.REGULAR((2,)),
        ],
        compiler_params=pltpu.CompilerParams(
            collective_id=0, has_side_effects=True, vmem_limit_bytes=56 << 20
        ),
        name="graph_layers",
    )(
        feats.T,
        cotangent.T,
        w_first,
        w_second,
        block_vals.reshape(ROWS * MINE, BLK, BLK),
        block_cols,
        block_count,
    )
    at = ROWS * BLK
    return (out[:, :at].T, out[:, at + F :].T, out[:, at : at + F].T)


def solution(mesh):
    return jax.shard_map(
        body,
        mesh=mesh,
        in_specs=(
            P("dom", "col"),
            P(),
            P(),
            P("dom", None),
            P("dom"),
            P("dom", "col", None, None),
            P("dom", "col"),
        ),
        out_specs=(P("dom", "col"), P(None, "col"), P(None, "col")),
        check_vma=False,
    )
```
